32 devices in a mesh: dp: 4 (over x, core), mp: 8 (over z, y).
Axes of the slice: x: 2, y: 2, z: 4, core: 2. Of those that a mesh axis runs over, the one named last changes fastest.
Arguments:
- hidden: bfloat16 [1536, 26624], P('dp', 'mp'), may hold values from -6 to 6
- down_weight: bfloat16 [26624, 8192], P('mp', 'dp'), may hold values from -0.0390625 to 0.0390625
- adapter_down: bfloat16 [16, 26624, 64], P('dp', 'mp'), may hold values from -0.0390625 to 0.0390625
- adapter_up: bfloat16 [16, 64, 8192], P('dp', None, 'mp'), may hold values from -0.1875 to 0.1875
- output_grad: bfloat16 [1536, 8192], P('dp', 'mp'), may hold values from -6 to 6
- adapter_per_block: int32 [12], replicated, may hold values from 0 to 15, as said below
- live_rows: int32 [4], replicated, may hold values from 96 to 384, as said below
Outputs:
- layer_out: bfloat16 [1536, 8192], P('dp', 'mp')
- hidden_gradient: bfloat16 [1536, 26624], P('dp', 'mp')
- down_grad: bfloat16 [16, 26624, 64], P('dp', 'mp')
- up_grad: bfloat16 [16, 64, 8192], P('dp', None, 'mp')
The draws below stay inside these ranges and needn't reach their ends.
Inputs may be any that keep to these rules, and one draw needn't show every extreme that they name: `adapter_per_block`: adapter k is owned by index k // 4 of dp; the 3 blocks of one index of dp use adapters of 3 different owners. `live_rows`: some index of dp has all 384 rows live.
All inputs are finite; a program needn't handle non-finite values.
Results may differ from the reference program's by a relative error of at most 0.0055.
Values may be sent and summed in bfloat16 or wider, within the bound.
No kernel may reach another device: no remote copies, remote signals or barrier semaphores. Data moves between devices by JAX's collectives and lax.ppermute only.
A program may use at most 192 MiB of HBM per device.

```python
import jax
import jax.numpy as jnp

D = 8192
FF = 26624
R = 64
BLK = 128
BLK_DEV = 3
ADP_DEV = 4
ROWS_DEV = 384
TOKENS = 1536
ADAPTERS = 16
N_DP = 4


def draw_adapter_per_block(key, part):
    key = jax.random.fold_in(key, 11)
    primary_random_key, secondary_random_key, third_key = jax.random.split(key, 3)
    ownership_boost = jax.random.randint(primary_random_key, (N_DP,), 0, 4) * 400
    ranking_scores = jax.random.randint(secondary_random_key, (N_DP, N_DP), 0, 1000) + ownership_boost[None, :]
    row_index = jnp.arange(N_DP, dtype=jnp.int32)[:, None]
    col_index = jnp.arange(N_DP, dtype=jnp.int32)[None, :]
    forced = (row_index == 0) & (col_index == 0) | (row_index == N_DP - 1) & (col_index == N_DP - 1)
    ranking_scores = ranking_scores + jnp.where(forced, 100000, 0).astype(jnp.int32)
    distinct = ranking_scores * N_DP + col_index
    ranked = jnp.argsort(-distinct, axis=1)[:, :BLK_DEV].astype(jnp.int32)
    local_selection = jax.random.randint(third_key, (N_DP, BLK_DEV), 0, ADP_DEV)
    slot_index = jnp.arange(BLK_DEV, dtype=jnp.int32)[None, :]
    local_selection = jnp.where((row_index == 0) & (slot_index == 0), 0, local_selection)
    local_selection = jnp.where((row_index == N_DP - 1) & (slot_index == 0), ADP_DEV - 1, local_selection)
    return (ranked * ADP_DEV + local_selection).reshape(-1).astype(jnp.int32)


def draw_live_rows(key, part):
    key = jax.random.fold_in(key, 23)
    primary_random_key, secondary_random_key = jax.random.split(key)
    counts = jax.random.randint(primary_random_key, (N_DP,), ROWS_DEV // 4, ROWS_DEV + 1)
    chosen = jax.random.randint(secondary_random_key, (), 0, N_DP)
    return jnp.where(jnp.arange(N_DP, dtype=jnp.int32) == chosen, ROWS_DEV, counts).astype(jnp.int32)


def levels(stream_key, extent, cuts, least, high):
    gain, own = 1.0, jax.random.fold_in(stream_key, 6)
    for position, shards_of in cuts:
        steps = jnp.exp(jax.random.uniform(jax.random.fold_in(own, position), (shards_of,), jnp.float32, least / len(cuts), high / len(cuts)))
        gain = gain * jnp.repeat(steps, extent[position] // shards_of).reshape([-1 if axis == position else 1 for axis in range(len(extent))])
    return gain


def scatter_about(own_key, extent, scale, most, shards=(), kind=jnp.bfloat16):
    values = scale * jax.random.normal(own_key, extent, jnp.float32)
    if shards:
        values = values * levels(own_key, extent, shards, -0.22, 0.18)
    return jnp.clip(values, -most, most).astype(kind)


def setup_inputs(seed: int = 0) -> dict:
    key_list = jax.random.split(jax.random.key(seed), 8)
    return {
        "hidden": scatter_about(key_list[0], (TOKENS, FF), 1.0, 6.0, ((0, 4), (1, 8))),
        "down_weight": scatter_about(key_list[1], (FF, D), FF ** -0.5, 0.0390625, ((0, 8), (1, 4))),
        "adapter_down": scatter_about(key_list[2], (ADAPTERS, FF, R), FF ** -0.5, 0.0390625, ((0, 4), (1, 8))),
        "adapter_up": scatter_about(key_list[3], (ADAPTERS, R, D), (16 * R) ** -0.5, 0.1875, ((0, 4), (2, 8))),
        "output_grad": scatter_about(key_list[4], (TOKENS, D), 1.0, 6.0, ((0, 4), (1, 8))),
        "adapter_per_block": draw_adapter_per_block(jax.random.fold_in(key_list[7], 71), 0),
        "live_rows": draw_live_rows(jax.random.fold_in(key_list[7], 71), 0),
    }


def reference(hidden, down_weight, adapter_down, adapter_up, output_grad, adapter_per_block, live_rows):
    token_count = hidden.shape[0]
    row_count = token_count // N_DP
    block_total = adapter_per_block.shape[0]
    positions = jnp.arange(token_count, dtype=jnp.int32)
    limits = jnp.repeat(live_rows, row_count)
    live_mask = ((positions % row_count) < limits)[:, None]
    pick_down = adapter_down[adapter_per_block].astype(jnp.float32)
    pick_up = adapter_up[adapter_per_block].astype(jnp.float32)
    hid_blocks = hidden.reshape(block_total, BLK, FF).astype(jnp.float32)
    down_act = jnp.einsum('btf,bfr->btr', hid_blocks, pick_down).astype(jnp.bfloat16)
    base_out = jnp.dot(hidden, down_weight, preferred_element_type=jnp.float32)
    branch = jnp.einsum('btr,brd->btd', down_act.astype(jnp.float32), pick_up).reshape(token_count, D)
    layer_out = jnp.where(live_mask, base_out + branch, jnp.float32(0.0)).astype(jnp.bfloat16)
    masked_grad = jnp.where(live_mask, output_grad, jnp.zeros_like(output_grad))
    grad_blocks = masked_grad.reshape(block_total, BLK, D).astype(jnp.float32)
    up_act = jnp.einsum('btd,brd->btr', grad_blocks, pick_up).astype(jnp.bfloat16)
    base_back = jnp.dot(masked_grad, down_weight.T, preferred_element_type=jnp.float32)
    side_back = jnp.einsum('btr,bfr->btf', up_act.astype(jnp.float32), pick_down).reshape(token_count, FF)
    hidden_gradient = (base_back + side_back).astype(jnp.bfloat16)
    term_down = jnp.einsum('btf,btr->bfr', hid_blocks, up_act.astype(jnp.float32)).astype(jnp.bfloat16)
    term_up = jnp.einsum('btr,btd->brd', down_act.astype(jnp.float32), grad_blocks).astype(jnp.bfloat16)
    onehot = (adapter_per_block[:, None] == jnp.arange(ADAPTERS, dtype=jnp.int32)[None, :]).astype(jnp.float32)
    down_grad = jnp.einsum('bk,bfr->kfr', onehot, term_down.astype(jnp.float32)).astype(jnp.bfloat16)
    up_grad = jnp.einsum('bk,brd->krd', onehot, term_up.astype(jnp.float32)).astype(jnp.bfloat16)
    return layer_out, hidden_gradient, down_grad, up_grad
```

```python
import functools

import jax
import jax.numpy as jnp
from jax import lax
from jax.experimental import pallas as pl
from jax.experimental.pallas import tpu as pltpu
from jax.sharding import PartitionSpec as P

BLK = 128
F32 = jnp.float32
BF16 = jnp.bfloat16
VMEM_LIMIT = 44 * 1024 * 1024


def forward_kernel(ha_ref, hb_ref, w_ref, a_ref, *refs):
    y_ref, p_ref = refs[-2:]
    w = w_ref[...]
    for index, h_ref in enumerate((ha_ref, hb_ref)):
        y_ref[index, 0] = jnp.dot(h_ref[...], w, preferred_element_type=F32)

    @pl.when(pl.program_id(0) == 0)
    def _():
        a = a_ref[...]
        for index, h_ref in enumerate((ha_ref, hb_ref)):
            p_ref[index] = jnp.dot(h_ref[...], a, preferred_element_type=F32)


def forward_pair(pair, ha, hb, weight, factor, total, n_dp, q):
    rows, units = ha.shape
    cols = weight.shape[1]
    width = cols // q
    tile = min(512, width)
    per = width // tile
    rank = factor.shape[1]
    whole = lambda i: (0, 0)
    in_specs = [
        pl.BlockSpec((rows, units), whole),
        pl.BlockSpec((rows, units), whole),
        pl.BlockSpec((units, tile), lambda i: (0, i)),
        pl.BlockSpec((units, rank), whole),
    ]
    operands = [ha, hb, weight, factor]
    aliases = {}
    if total is not None:
        in_specs.append(pl.BlockSpec(memory_space=pl.ANY))
        operands.append(total)
        aliases = {4: 0}
    return pl.pallas_call(
        forward_kernel,
        grid=(cols // tile,),
        in_specs=in_specs,
        out_specs=[
            pl.BlockSpec((2, 1, rows, tile), lambda i: (pair, i // per, 0, i % per)),
            pl.BlockSpec((2, rows, rank), lambda i: (0, 0, 0)),
        ],
        out_shape=[
            jax.ShapeDtypeStruct((n_dp, q, rows, width), F32),
            jax.ShapeDtypeStruct((2, rows, rank), F32),
        ],
        input_output_aliases=aliases,
        cost_estimate=pl.CostEstimate(
            flops=4 * rows * units * (cols + rank),
            bytes_accessed=2 * units * (cols + rank + 2 * rows) + 8 * rows * cols,
            transcendentals=0,
        ),
        compiler_params=pltpu.CompilerParams(vmem_limit_bytes=VMEM_LIMIT),
        name="forward_pair",
    )(*operands)


def backward_kernel(q, g_ref, u_ref, w_ref, a_ref, z_ref):
    width = g_ref.shape[3]
    turned = (((1,), (1,)), ((), ()))
    acc = lax.dot_general(u_ref[...], a_ref[...], turned, preferred_element_type=F32)
    for h in range(q):
        acc += lax.dot_general(
            g_ref[0, h], w_ref[:, h * width : (h + 1) * width], turned, preferred_element_type=F32
        )
    z_ref[...] = acc.astype(z_ref.dtype)


def backward_part(slot, grads, acts, weight, factor, dtype):
    _, q, rows, width = grads.shape
    units, cols = weight.shape
    rank = factor.shape[1]
    tile = 256 if units % 256 == 0 else units
    return pl.pallas_call(
        functools.partial(backward_kernel, q),
        grid=(units // tile,),
        in_specs=[
            pl.BlockSpec((1, q, rows, width), lambda i: (slot, 0, 0, 0)),
            pl.BlockSpec((rows, rank), lambda i: (0, 0)),
            pl.BlockSpec((tile, cols), lambda i: (i, 0)),
            pl.BlockSpec((tile, rank), lambda i: (i, 0)),
        ],
        out_specs=pl.BlockSpec((rows, tile), lambda i: (0, i)),
        out_shape=jax.ShapeDtypeStruct((rows, units), dtype),
        cost_estimate=pl.CostEstimate(
            flops=2 * rows * units * (cols + rank),
            bytes_accessed=2 * (units + rows) * (cols + rank) + 4 * rows * units,
            transcendentals=0,
        ),
        compiler_params=pltpu.CompilerParams(vmem_limit_bytes=VMEM_LIMIT),
        name="backward_part",
    )(grads, acts, weight, factor)


def shards(
    hidden, down_weight, adapter_down, adapter_up, output_grad, adapter_per_block, live_rows
):
    n_dp = lax.axis_size("dp")
    n_mp = lax.axis_size("mp")
    dp = lax.axis_index("dp")
    mp = lax.axis_index("mp")
    q = n_mp // n_dp
    rows, units = hidden.shape
    width = output_grad.shape[1]
    owned, _, rank = adapter_down.shape
    blocks = rows // BLK
    half = n_mp // 2
    top = rows // 2

    def exchange(value, bit, axis="dp"):
        count = n_dp if axis == "dp" else n_mp
        return lax.ppermute(value, axis, [(i, i ^ bit) for i in range(count)])

    def swap_places(value):
        pairs = [
            (j * n_mp + m, (m // q) * n_mp + j * q + m % q)
            for j in range(n_dp)
            for m in range(n_mp)
        ]
        return lax.ppermute(value, ("dp", "mp"), pairs)

    ring = list(range(0, n_mp, 2)) + list(range(n_mp - 1, 0, -2))
    up_ring = [(ring[i], ring[(i + 1) % n_mp]) for i in range(n_mp)]
    down_ring = [(b, a) for a, b in up_ring]
    place = jnp.where(mp % 2 == 0, mp // 2, n_mp - 1 - mp // 2)

    def ring_slot(offset):
        at = (place + offset) % n_mp
        index = jnp.where(at < half, 2 * at, 2 * (n_mp - 1 - at) + 1)
        return (index // q) ^ dp, index % q

    def onward(value):
        return lax.ppermute(value, "mp", up_ring)

    def backward_on(value):
        return lax.ppermute(value, "mp", down_ring)

    id_table = adapter_per_block.reshape(n_dp, blocks)
    ids_of = [lax.dynamic_index_in_dim(id_table, dp ^ r, 0, False) for r in range(n_dp)]
    my_ids = dp * owned + jnp.arange(owned, dtype=jnp.int32)
    mine = [ids[:, None] == my_ids[None, :] for ids in ids_of]
    live_count = lax.dynamic_index_in_dim(live_rows, dp, 0, False)
    live_mask = (jnp.arange(rows, dtype=jnp.int32) < live_count)[:, None]
    masked_grad = jnp.where(live_mask, output_grad, jnp.zeros_like(output_grad))

    swapped = swap_places(masked_grad)

    hid = {0: hidden}
    bit = 2
    while bit < n_dp:
        for r in list(hid):
            hid[r ^ bit] = exchange(hid[r], bit)
        bit *= 2
    for r in list(hid):
        hid[r ^ 1] = exchange(hid[r], 1)

    def for_partner(r):
        local = jnp.sum(
            jnp.where(mine[r], jnp.arange(owned, dtype=jnp.int32)[None, :], 0), dtype=jnp.int32
        )
        return lax.dynamic_index_in_dim(adapter_up, local, 0, False)

    arrived_up = jnp.stack(
        [for_partner(0)] + [exchange(for_partner(r), r) for r in range(1, n_dp)]
    )
    own_owner = ids_of[0] // owned
    block_up = jnp.stack(
        [
            lax.dynamic_index_in_dim(arrived_up, own_owner[b] ^ dp, 0, False)
            for b in range(blocks)
        ]
    )
    grad_blocks = masked_grad.reshape(blocks, BLK, width)

    def sum_over_mp(value):
        step = 1
        while step < n_mp:
            value = value + exchange(value, step, "mp")
            step *= 2
        return value

    up_act = sum_over_mp(
        jnp.einsum("brd,btd->brt", block_up, grad_blocks, preferred_element_type=F32)
    ).astype(BF16)

    def spread(act, r):
        act = jnp.transpose(act, (0, 2, 1))
        picked = jnp.where(mine[r][:, None, :, None], act[:, :, None, :], jnp.zeros((), BF16))
        return picked.reshape(rows, owned * rank)

    acts = [spread(up_act if r == 0 else exchange(up_act, r), r) for r in range(n_dp)]

    grads = jnp.zeros((n_dp, q, rows, width), BF16)

    def put(grads, offset, value, row):
        group, part = ring_slot(offset)
        return lax.dynamic_update_slice(grads, value[None, None], (group, part, row, 0))

    ahead = behind = swapped
    grads = put(grads, 0, swapped, 0)
    for step in range(1, half):
        ahead = onward(ahead)
        behind = backward_on(behind)
        grads = put(grads, -step, ahead, 0)
        grads = put(grads, step, behind, 0)
    grads = put(grads, half, onward(ahead[:top]), 0)
    grads = put(grads, half, backward_on(behind[top:]), top)

    factor = jnp.transpose(adapter_down, (1, 0, 2)).reshape(units, owned * rank)
    total = None
    down_parts = []
    for pair in range(n_dp // 2):
        total, part = forward_pair(
            pair, hid[2 * pair], hid[2 * pair + 1], down_weight, factor, total, n_dp, q
        )
        down_parts += [part[0], part[1]]

    def pick(part, r):
        part = part.reshape(blocks, BLK, owned, rank)
        part = jnp.sum(jnp.where(mine[r][:, None, :, None], part, F32(0.0)), axis=2)
        return jnp.transpose(part, (0, 2, 1))

    down_sum = pick(down_parts[0], 0)
    for r in range(1, n_dp):
        down_sum = down_sum + exchange(pick(down_parts[r], r), r)
    down_act = sum_over_mp(down_sum).astype(BF16)

    def chunk(offset):
        group, part = ring_slot(offset)
        return lax.dynamic_slice(total, (group, part, 0, 0), (1, 1, rows, width))[0, 0]

    far = chunk(half)
    ahead = onward(far[:top].astype(BF16)).astype(F32)
    behind = backward_on(far[top:].astype(BF16)).astype(F32)
    ahead = jnp.pad(ahead, ((0, rows - top), (0, 0)))
    behind = jnp.pad(behind, ((top, 0), (0, 0)))
    for step in range(half - 1, 0, -1):
        ahead = onward((chunk(step) + ahead).astype(BF16)).astype(F32)
        behind = backward_on((chunk(-step) + behind).astype(BF16)).astype(F32)
    base_out = swap_places((chunk(0) + ahead + behind).astype(BF16))

    branch = jnp.einsum(
        "brt,brd->btd", down_act, block_up, preferred_element_type=F32
    ).reshape(rows, width)
    layer_out = jnp.where(live_mask, base_out.astype(F32) + branch, F32(0.0)).astype(BF16)

    parts = {}
    for r in range(n_dp - 1, -1, -1):
        parts[r] = backward_part(
            r, grads, acts[r], down_weight, factor, BF16 if r % 2 else F32
        )
    bit = 1
    while bit < n_dp:
        for r in [r for r in parts if r & bit]:
            arrived = exchange(parts.pop(r).astype(BF16), bit)
            parts[r ^ bit] = parts[r ^ bit] + arrived.astype(F32)
        bit *= 2
    hidden_gradient = parts[0].astype(BF16)

    down_grad = sum(
        lax.dot_general(
            hid[r], acts[r], (((0,), (0,)), ((), ())), preferred_element_type=F32
        )
        for r in range(n_dp)
    )
    down_grad = jnp.transpose(down_grad.reshape(units, owned, rank), (1, 0, 2)).astype(BF16)

    term_up = jnp.einsum(
        "brt,btd->brd", down_act, grad_blocks, preferred_element_type=F32
    ).astype(BF16)

    def term_for(r):
        chosen = (own_owner == (dp ^ r))[:, None, None]
        return jnp.sum(jnp.where(chosen, term_up, jnp.zeros((), BF16)).astype(F32), axis=0).astype(
            BF16
        )

    up_grad = jnp.zeros((owned, rank, width), F32)
    for r in range(n_dp):
        term = term_for(r)
        if r:
            term = exchange(term, r)
        uses = jnp.any(mine[r], axis=0)[:, None, None]
        up_grad = up_grad + jnp.where(uses, term[None].astype(F32), F32(0.0))
    return layer_out, hidden_gradient, down_grad, up_grad.astype(BF16)


def solution(mesh):
    return jax.shard_map(
        shards,
        mesh=mesh,
        in_specs=(
            P("dp", "mp"),
            P("mp", "dp"),
            P("dp", "mp", None),
            P("dp", None, "mp"),
            P("dp", "mp"),
            P(),
            P(),
        ),
        out_specs=(P("dp", "mp"), P("dp", "mp"), P("dp", "mp", None), P("dp", None, "mp")),
        check_vma=False,
    )
```

```python
import functools

import jax
import jax.numpy as jnp
from jax import lax
from jax.experimental import pallas as pl
from jax.experimental.pallas import tpu as pltpu
from jax.sharding import PartitionSpec as P

BLK = 128
F32 = jnp.float32
BF16 = jnp.bfloat16
VMEM_LIMIT = 44 * 1024 * 1024


TURNED = (((1,), (1,)), ((), ()))
FIRSTS = (((0,), (0,)), ((), ()))


def params():
    return pltpu.CompilerParams(vmem_limit_bytes=VMEM_LIMIT)


def whole(shape):
    return pl.BlockSpec(shape, lambda *_: (0,) * len(shape))


def call(kernel, name, scalars, operands, out_shapes, scratch_shapes=()):
    return pl.pallas_call(
        kernel,
        grid_spec=pltpu.PrefetchScalarGridSpec(
            num_scalar_prefetch=len(scalars),
            grid=(1,),
            in_specs=[whole(x.shape) for x in operands],
            out_specs=[whole(x.shape) for x in out_shapes],
            scratch_shapes=list(scratch_shapes),
        ),
        out_shape=list(out_shapes),
        compiler_params=params(),
        name=name,
    )(*scalars, *operands)


def mask_kernel(at_ref, live_ref, grad_ref, out_ref):
    row = lax.broadcasted_iota(jnp.int32, grad_ref.shape, 0)
    grad = grad_ref[...]
    out_ref[...] = jnp.where(row < live_ref[at_ref[0]], grad, jnp.zeros_like(grad))


def select_kernel(n_dp, owned, rank, at_ref, id_ref, up_ref, *out_refs):
    mask_ref = out_refs[-1]
    dp = at_ref[0]
    blocks = mask_ref.shape[1]
    column = lax.broadcasted_iota(jnp.int32, (BLK, owned * rank), 1)
    for r in range(n_dp):
        chosen = jnp.int32(0)
        for b in range(blocks):
            local = id_ref[(dp ^ r) * blocks + b] - dp * owned
            chosen = jnp.where((local >= 0) & (local < owned), local, chosen)
            hit = (column >= local * rank) & (column < (local + 1) * rank)
            mask_ref[r, b] = jnp.where(hit, 1.0, 0.0).astype(BF16)
        out_refs[r][...] = up_ref[chosen]


def up_kernel(n_dp, owned, at_ref, id_ref, grad_ref, *refs):
    part_ref, block_ref = refs[n_dp:]
    dp = at_ref[0]
    blocks, rank, _ = block_ref.shape
    for b in range(blocks):
        source = (id_ref[dp * blocks + b] // owned) ^ dp
        for r in range(n_dp):

            @pl.when(source == r)
            def _():
                block_ref[b] = refs[r][...]

    for b in range(blocks):
        part_ref[b * rank : (b + 1) * rank, :] = lax.dot_general(
            block_ref[b],
            grad_ref[b * BLK : (b + 1) * BLK, :],
            TURNED,
            preferred_element_type=F32,
        )


def term_kernel(
    n_dp, owned, at_ref, id_ref, live_ref, down_ref, grad_ref, block_ref, branch_ref, *out_refs
):
    dp = at_ref[0]
    blocks, rank, width = block_ref.shape
    down_act = down_ref[...].astype(BF16)
    row = lax.broadcasted_iota(jnp.int32, (BLK, width), 0)
    for r in range(n_dp):
        out_refs[r][...] = jnp.zeros(out_refs[r].shape, BF16)
    for b in range(blocks):
        rows = slice(b * BLK, (b + 1) * BLK)
        act = down_act[b * rank : (b + 1) * rank]
        branch = lax.dot_general(act, block_ref[b], FIRSTS, preferred_element_type=F32)
        branch_ref[rows, :] = jnp.where(row + b * BLK < live_ref[dp], branch, 0.0)
        term = jnp.dot(act, grad_ref[rows, :], preferred_element_type=F32).astype(BF16)
        owner = (id_ref[dp * blocks + b] // owned) ^ dp
        for r in range(n_dp):

            @pl.when(owner == r)
            def _():
                out_refs[r][...] = term


def up_grad_kernel(n_dp, blocks, at_ref, id_ref, *refs):
    out_ref = refs[n_dp]
    dp = at_ref[0]
    owned = out_ref.shape[0]
    for a in range(owned):
        total = jnp.zeros(out_ref.shape[1:], F32)
        for r in range(n_dp):
            uses = jnp.int32(0)
            for b in range(blocks):
                uses += (id_ref[(dp ^ r) * blocks + b] == dp * owned + a).astype(jnp.int32)
            total += jnp.where(uses > 0, refs[r][...].astype(F32), 0.0)
        out_ref[a] = total.astype(BF16)


def ring_slot(offset, at, n_dp, n_mp):
    dp, mp = at[0], at[1]
    place = jnp.where(mp % 2 == 0, mp // 2, n_mp - 1 - mp // 2)
    there = (place + offset + n_mp) % n_mp
    index = jnp.where(there < n_mp // 2, 2 * there, 2 * (n_mp - 1 - there) + 1)
    q = n_mp // n_dp
    return (index // q) ^ dp, index % q


def add_kernel(at_ref, a_ref, b_ref, ahead_ref, behind_ref, a_out, b_out):
    a_out[...] = (a_ref[0, 0].astype(F32) + ahead_ref[...].astype(F32)).astype(BF16)
    b_out[...] = (b_ref[0, 0].astype(F32) + behind_ref[...].astype(F32)).astype(BF16)


def half_add_kernel(at_ref, a_ref, b_ref, ahead_ref, behind_ref, a_out, b_out):
    first = pl.program_id(0) == 0

    @pl.when(first)
    def _():
        a_out[...] = (a_ref[0, 0].astype(F32) + ahead_ref[...].astype(F32)).astype(BF16)
        b_out[...] = b_ref[0, 0]

    @pl.when(jnp.logical_not(first))
    def _():
        a_out[...] = a_ref[0, 0]
        b_out[...] = (b_ref[0, 0].astype(F32) + behind_ref[...].astype(F32)).astype(BF16)


def ring_add(step, at, total, ahead, behind, n_mp, halves):
    n_dp, _, rows, width = total.shape
    top = rows // 2

    def slot(offset):
        def index(i, at_ref):
            group, part = ring_slot(offset, at_ref, n_dp, n_mp)
            return group, part, i, 0

        return pl.BlockSpec((1, 1, top, width), index)

    arrived = pl.BlockSpec((top, width), lambda i, at_ref: (0 if halves else i, 0))
    sent = pl.BlockSpec((top, width), lambda i, at_ref: (i, 0))
    return pl.pallas_call(
        half_add_kernel if halves else add_kernel,
        grid_spec=pltpu.PrefetchScalarGridSpec(
            num_scalar_prefetch=1,
            grid=(2,),
            in_specs=[slot(step), slot(-step), arrived, arrived],
            out_specs=[sent, sent],
        ),
        out_shape=[jax.ShapeDtypeStruct((rows, width), BF16)] * 2,
        compiler_params=params(),
        name="ring_add",
    )(at, total, total, ahead, behind)


def opposite_kernel(at_ref, total_ref, first_ref, second_ref):
    top = first_ref.shape[0]
    first_ref[...] = total_ref[0, 0, :top]
    second_ref[...] = total_ref[0, 0, top:]


def opposite(at, total, n_mp):
    n_dp, _, rows, width = total.shape

    def index(i, at_ref):
        group, part = ring_slot(n_mp // 2, at_ref, n_dp, n_mp)
        return group, part, 0, 0

    out = pl.BlockSpec((rows // 2, width), lambda i, at_ref: (0, 0))
    return pl.pallas_call(
        opposite_kernel,
        grid_spec=pltpu.PrefetchScalarGridSpec(
            num_scalar_prefetch=1,
            grid=(1,),
            in_specs=[pl.BlockSpec((1, 1, rows, width), index)],
            out_specs=[out, out],
        ),
        out_shape=[jax.ShapeDtypeStruct((rows // 2, width), BF16)] * 2,
        compiler_params=params(),
        name="opposite",
    )(at, total)


def last_add_kernel(n_dp, n_mp, at_ref, live_ref, own_ref, ahead_ref, behind_ref, out_ref):
    total = own_ref[0, 0].astype(F32) + ahead_ref[...].astype(F32) + behind_ref[...].astype(F32)
    row = lax.broadcasted_iota(jnp.int32, total.shape, 0) + pl.program_id(0) * total.shape[0]
    live = live_ref[at_ref[1] // (n_mp // n_dp)]
    out_ref[...] = jnp.where(row < live, total, 0.0).astype(BF16)


def last_add(at, live_rows, total, ahead, behind, n_mp):
    n_dp, _, rows, width = total.shape

    def index(i, at_ref, live_ref):
        group, part = ring_slot(0, at_ref, n_dp, n_mp)
        return group, part, i, 0

    half = pl.BlockSpec((rows // 2, width), lambda i, at_ref, live_ref: (i, 0))
    return pl.pallas_call(
        functools.partial(last_add_kernel, n_dp, n_mp),
        grid_spec=pltpu.PrefetchScalarGridSpec(
            num_scalar_prefetch=2,
            grid=(2,),
            in_specs=[pl.BlockSpec((1, 1, rows // 2, width), index), half, half],
            out_specs=half,
        ),
        out_shape=jax.ShapeDtypeStruct((rows, width), BF16),
        compiler_params=params(),
        name="last_add",
    )(at, live_rows, total, ahead, behind)


def combine_kernel(own_ref, *refs):
    total = own_ref[...]
    for ref in refs[:-2]:
        total += ref[...].astype(F32)
    refs[-1][...] = total.astype(BF16)


def combine(start, own, near, arrived, out):
    rows, units = own.shape
    tile = 32
    first = start // tile
    placed = pl.BlockSpec((tile, units), lambda i: (i + first, 0))
    piece = pl.BlockSpec((tile, units), lambda i: (i, 0))
    return pl.pallas_call(
        combine_kernel,
        grid=(arrived[0].shape[0] // tile,),
        in_specs=[placed, placed]
        + [piece] * len(arrived)
        + [pl.BlockSpec(memory_space=pl.ANY)],
        out_specs=placed,
        out_shape=jax.ShapeDtypeStruct((rows, units), BF16),
        input_output_aliases={2 + len(arrived): 0},
        compiler_params=params(),
        name="combine",
    )(own, near, *arrived, out)


def blank_kernel(out_ref):
    pass


def blank(shape, dtype):
    return pl.pallas_call(
        blank_kernel,
        out_specs=pl.BlockSpec(memory_space=pl.ANY),
        out_shape=jax.ShapeDtypeStruct(shape, dtype),
        name="blank",
    )()


def forward_kernel(count, *refs):
    w_ref, a_ref, m_ref = refs[count : count + 3]
    y_ref, p_ref = refs[-2:]
    hid = jnp.concatenate([ref[...] for ref in refs[:count]], axis=0)
    out = jnp.dot(hid, w_ref[...], preferred_element_type=F32).astype(BF16)
    groups, _, blocks, _, tile = y_ref.shape
    y_ref[:, 0] = out.reshape(groups, blocks, BLK, tile)

    @pl.when(pl.program_id(0) == 0)
    def _():
        ranks = a_ref.shape[1]
        rank = p_ref.shape[1] // blocks
        part = jnp.dot(hid, a_ref[...], preferred_element_type=F32)
        part = jnp.where(m_ref[...].reshape(part.shape) > 0, part, 0.0)
        picked = part[:, :rank]
        for a in range(1, ranks // rank):
            picked = picked + part[:, a * rank : (a + 1) * rank]
        picked = picked.astype(BF16)
        row = lax.broadcasted_iota(jnp.int32, (BLK, BLK), 0)
        column = lax.broadcasted_iota(jnp.int32, (BLK, BLK), 1)
        unit = jnp.where(row == column, 1.0, 0.0).astype(BF16)
        for g in range(groups):
            for b in range(blocks):
                start = (g * blocks + b) * BLK
                p_ref[g, b * rank : (b + 1) * rank, :] = lax.dot_general(
                    picked[start : start + BLK], unit, FIRSTS, preferred_element_type=F32
                ).astype(BF16)


def forward_part(groups, blocks, hids, weight, factor, masks, total, q, rank):
    units, cols = weight.shape
    n_dp, all_blocks, _, ranks = masks.shape
    width = cols // q
    tile = min(512, width)
    per = width // tile
    group, block = groups[0] // groups[1], blocks[0] // blocks[1]
    in_specs = [whole(hid.shape) for hid in hids] + [
        pl.BlockSpec((units, tile), lambda i: (0, i)),
        whole((units, ranks)),
        pl.BlockSpec((groups[1], blocks[1], BLK, ranks), lambda i: (group, block, 0, 0)),
    ]
    operands = [*hids, weight, factor, masks]
    aliases = {}
    if total is not None:
        aliases = {len(operands): 0}
        in_specs.append(pl.BlockSpec(memory_space=pl.ANY))
        operands.append(total)
    turned = (groups[1], blocks[1] * rank, BLK)
    return pl.pallas_call(
        functools.partial(forward_kernel, len(hids)),
        grid=(cols // tile,),
        in_specs=in_specs,
        out_specs=[
            pl.BlockSpec(
                (groups[1], 1, blocks[1], BLK, tile),
                lambda i: (group, i // per, block, 0, i % per),
            ),
            whole(turned),
        ],
        out_shape=[
            jax.ShapeDtypeStruct((n_dp, q, all_blocks, BLK, width), BF16),
            jax.ShapeDtypeStruct(turned, BF16),
        ],
        input_output_aliases=aliases,
        compiler_params=params(),
        name="forward_part",
    )(*operands)


def spread(act, mask):
    blocks, _, ranks = mask.shape
    rank = act.shape[0] // blocks
    row = lax.broadcasted_iota(jnp.int32, (rank, ranks), 0)
    column = lax.broadcasted_iota(jnp.int32, (rank, ranks), 1)
    repeat = jnp.where(column % rank == row, 1.0, 0.0).astype(BF16)
    wide = [
        lax.dot_general(
            act[b * rank : (b + 1) * rank], repeat, FIRSTS, preferred_element_type=F32
        )
        for b in range(blocks)
    ]
    wide = jnp.concatenate(wide, axis=0)
    return jnp.where(mask.reshape(wide.shape) > 0, wide, 0.0).astype(BF16)


def backward_kernel(groups, n_mp, offsets, at_ref, *refs):
    first, count = groups
    slots = len(offsets)
    block_refs = refs[: slots + 1]
    act_refs = refs[slots + 1 : slots + 1 + count]
    m_ref, w_ref, a_ref = refs[slots + 1 + count : slots + 4 + count]
    z_refs = refs[slots + 4 + count : -3]
    g_ref, u_ref, sems = refs[-3:]
    _, q, rows, _ = g_ref.shape
    n_dp = n_mp // q
    top = rows // 2

    def transfers(act):
        for index in range(slots + 1):
            there, part = ring_slot(offsets[min(index, slots - 1)], at_ref, n_dp, n_mp)
            target = g_ref.at[there % count, part]
            if index >= slots - 1:
                target = target.at[pl.ds(top * (index - slots + 1), top)]
            copy = pltpu.make_async_copy(block_refs[index], target, sems.at[index])
            pl.when(there // count == first // count)(copy.start if act else copy.wait)

    @pl.when(pl.program_id(0) == 0)
    def _():
        transfers(True)
        for g in range(count):
            u_ref[g * rows : (g + 1) * rows, :] = spread(act_refs[g][...], m_ref[g])
        transfers(False)

    grads = [
        jnp.concatenate([g_ref[g, h] for h in range(q)], axis=1) for g in range(count)
    ]
    out = lax.dot_general(
        jnp.concatenate(grads, axis=0), w_ref[...], TURNED, preferred_element_type=F32
    )
    out += jnp.dot(u_ref[...], a_ref[...], preferred_element_type=F32)
    for g in range(count):
        z_refs[g][...] = out[g * rows : (g + 1) * rows].astype(z_refs[g].dtype)


def backward_part(groups, at, blocks, offsets, acts, masks, weight, turned_factor, n_mp):
    units, cols = weight.shape
    n_dp, parts, _, ranks = masks.shape
    rows = parts * BLK
    q = n_mp // n_dp
    first, count = groups
    tile = min(896, units)
    return pl.pallas_call(
        functools.partial(backward_kernel, groups, n_mp, offsets),
        grid_spec=pltpu.PrefetchScalarGridSpec(
            num_scalar_prefetch=1,
            grid=(pl.cdiv(units, tile),),
            in_specs=[pl.BlockSpec(memory_space=pl.ANY)] * len(blocks)
            + [whole(act.shape) for act in acts]
            + [
                pl.BlockSpec(
                    (count, parts, BLK, ranks), lambda i, at_ref: (first // count, 0, 0, 0)
                ),
                pl.BlockSpec((tile, cols), lambda i, at_ref: (i, 0)),
                pl.BlockSpec((ranks, tile), lambda i, at_ref: (0, i)),
            ],
            out_specs=[pl.BlockSpec((rows, tile), lambda i, at_ref: (0, i))] * count,
            scratch_shapes=[
                pltpu.VMEM((count, q, rows, cols // q), BF16),
                pltpu.VMEM((count * rows, ranks), BF16),
                pltpu.SemaphoreType.DMA((len(blocks),)),
            ],
        ),
        out_shape=[
            jax.ShapeDtypeStruct((rows, units), BF16 if (first + g) % 2 else F32)
            for g in range(count)
        ],
        compiler_params=params(),
        name="backward_part",
    )(at, *blocks, *acts, masks, weight, turned_factor)


def factor_grad_kernel(n_dp, m_ref, *refs):
    acts = [spread(refs[r][...], m_ref[r]) for r in range(n_dp)]
    hid = jnp.concatenate([ref[...] for ref in refs[n_dp:-1]], axis=0)
    out = lax.dot_general(
        jnp.concatenate(acts, axis=0), hid, FIRSTS, preferred_element_type=F32
    )
    refs[-1][...] = out.astype(BF16)


def factor_grad(masks, acts, hids):
    ranks = masks.shape[3]
    units = hids[0].shape[1]
    tile = units // 2 if units % 256 == 0 else units
    return pl.pallas_call(
        functools.partial(factor_grad_kernel, len(acts)),
        grid=(units // tile,),
        in_specs=[whole(masks.shape)]
        + [whole(act.shape) for act in acts]
        + [pl.BlockSpec((hid.shape[0], tile), lambda i: (0, i)) for hid in hids],
        out_specs=pl.BlockSpec((ranks, tile), lambda i: (0, i)),
        out_shape=jax.ShapeDtypeStruct((ranks, units), BF16),
        compiler_params=params(),
        name="factor_grad",
    )(masks, *acts, *hids)


def shards(
    hidden, down_weight, adapter_down, adapter_up, output_grad, adapter_per_block, live_rows
):
    n_dp = lax.axis_size("dp")
    n_mp = lax.axis_size("mp")
    at = jnp.stack([lax.axis_index("dp"), lax.axis_index("mp")])
    q = n_mp // n_dp
    rows, units = hidden.shape
    width = output_grad.shape[1]
    owned, _, rank = adapter_down.shape
    blocks = rows // BLK
    half = n_mp // 2
    top = rows // 2
    fence = lambda *values: lax.optimization_barrier(values)
    like = jax.ShapeDtypeStruct

    def exchange(value, bit, axis="dp"):
        count = n_dp if axis == "dp" else n_mp
        return lax.ppermute(value, axis, [(i, i ^ bit) for i in range(count)])

    def swap_places(value):
        pairs = [
            (j * n_mp + m, (m // q) * n_mp + j * q + m % q)
            for j in range(n_dp)
            for m in range(n_mp)
        ]
        return lax.ppermute(value, ("dp", "mp"), pairs)

    ring = list(range(0, n_mp, 2)) + list(range(n_mp - 1, 0, -2))
    up_ring = [(ring[i], ring[(i + 1) % n_mp]) for i in range(n_mp)]
    down_ring = [(b, a) for a, b in up_ring]

    def onward(value):
        return lax.ppermute(value, "mp", up_ring)

    def backward_on(value):
        return lax.ppermute(value, "mp", down_ring)

    evens = range(2, n_dp, 2)

    def fetch(hidden, piece):
        held = {0: hidden[piece * BLK : (piece + 1) * BLK]}
        bit = 2
        while bit < n_dp:
            for r in list(held):
                held[r ^ bit] = exchange(held[r], bit)
            bit *= 2
        return {r: held[r] for r in evens}

    def pass_on(fetched):
        return {r + 1: exchange(fetched[r], 1) for r in evens}

    far_steps = [1 << k for k in range(n_mp.bit_length() - 2, -1, -1)]
    sum_steps = [far_steps[:-2], far_steps[-2:-1], far_steps[-1:]]

    def sum_step(value, index):
        for bit in sum_steps[index]:
            value = value + exchange(value.astype(BF16), bit, "mp").astype(F32)
        return value

    (masked_grad,) = call(
        mask_kernel, "mask", [at, live_rows], [output_grad], [like(output_grad.shape, BF16)]
    )
    swapped = swap_places(masked_grad)
    near = exchange(hidden, 1)
    adapter_up, masked_grad, at = fence(adapter_up, masked_grad, at)
    *chosen, masks = call(
        functools.partial(select_kernel, n_dp, owned, rank),
        "select",
        [at, adapter_per_block],
        [adapter_up],
        [like((rank, width), BF16)] * n_dp + [like((n_dp, blocks, BLK, owned * rank), BF16)],
    )
    arrived_up = [exchange(chosen[r], r) if r else chosen[0] for r in range(n_dp)]
    arrived_up[1], hidden_0 = fence(arrived_up[1], hidden)
    fetched = [fetch(hidden_0, 0)]
    turned_factor = jnp.transpose(adapter_down, (0, 2, 1)).reshape(owned * rank, units)
    factor = turned_factor.T

    def forward(groups, span, hids, total):
        return forward_part(groups, span, hids, down_weight, factor, masks, total, q, rank)

    picked = {}
    total, own = forward((0, 1), (0, blocks), [hidden], None)
    picked[0] = [own[0]]
    arrived_up, total, hidden = fence(arrived_up, total, hidden)
    up_sum, block_up = call(
        functools.partial(up_kernel, n_dp, owned),
        "up_part",
        [at, adapter_per_block],
        [masked_grad, *arrived_up],
        [like((blocks * rank, BLK), F32), like((blocks, rank, width), BF16)],
    )
    up_sum = sum_step(up_sum, 0)
    swapped, near, fetched[0], total, up_sum, hidden = fence(
        swapped, near, fetched[0], total, up_sum, hidden
    )

    ahead = behind = swapped
    ring_blocks = [swapped]
    offsets = [0] + [sign * step for step in range(1, half) for sign in (-1, 1)] + [half]
    ahead, behind = onward(ahead), backward_on(behind)
    fetched.append(fetch(hidden, 1))
    passed = [pass_on(fetched[0])]
    up_sum = sum_step(up_sum, 1)
    total, own = forward((1, 1), (0, blocks), [near], total)
    picked[1] = [own[0]]
    ahead, behind, fetched[1], passed, total, up_sum, hidden = fence(
        ahead, behind, fetched[1], passed, total, up_sum, hidden
    )
    ring_blocks += [ahead, behind]
    ahead, behind = onward(ahead), backward_on(behind)
    fetched.append(fetch(hidden, 2))
    passed.append(pass_on(fetched[1]))
    up_sum = sum_step(up_sum, 2)

    def forward_pairs(span, total):
        pieces = range(span[0], span[0] + span[1])
        for r in evens:
            hids = [fetched[p][r] for p in pieces] + [passed[p][r + 1] for p in pieces]
            total, pair = forward((r, 2), span, hids, total)
            for g in range(2):
                picked.setdefault(r + g, []).append(pair[g])
        return total

    total = forward_pairs((0, 2), total)
    ahead, behind, fetched[2], passed, total, up_sum = fence(
        ahead, behind, fetched[2], passed, total, up_sum
    )
    ring_blocks += [ahead, behind]
    for _ in range(3, half):
        ahead, behind = onward(ahead), backward_on(behind)
        ring_blocks += [ahead, behind]
    passed.append(pass_on(fetched[2]))
    passed, up_act = fence(passed, up_sum.astype(BF16))
    acts = [exchange(up_act, r) if r else up_act for r in range(n_dp)]
    total = forward_pairs((2, 1), total)
    ahead, behind, acts, total, picked = fence(ahead, behind, acts, total, picked)
    ring_blocks[-2:] = [ahead, behind]
    total = total.reshape(n_dp, q, rows, width)

    last = [onward(ahead[:top]), backward_on(behind[top:])]
    ahead, behind = opposite(at, total, n_mp)
    ahead, behind = onward(ahead), backward_on(behind)
    held = {r: jnp.concatenate(picked[r], axis=0) for r in range(n_dp)}
    bit = 1
    while bit < n_dp:
        sent = [r for r in held if r & bit]
        arrived = exchange(jnp.concatenate([held.pop(r).astype(BF16) for r in sent]), bit)
        for index, r in enumerate(sent):
            size = blocks * rank
            piece = arrived[index * size : (index + 1) * size]
            held[r ^ bit] = held[r ^ bit].astype(F32) + piece.astype(F32)
        bit *= 2
    down_sum = held[0]
    last, ahead, behind, down_sum, acts = fence(last, ahead, behind, down_sum, acts)
    ring_blocks += last

    def backward(first, count, acts):
        return backward_part(
            (first, count),
            at,
            ring_blocks,
            offsets,
            acts[first : first + count],
            masks,
            down_weight,
            turned_factor,
            n_mp,
        )

    def add_and_send(step, ahead, behind, acts, halves=False):
        ahead, behind = ring_add(step, at, total, ahead, behind, n_mp, halves)
        ahead, behind, acts = fence(ahead, behind, acts)
        return onward(ahead), backward_on(behind), acts

    ends = [0, rows // 3, 3 * rows // 4, rows]

    def partial_gradient(piece):
        cut = slice(ends[piece], ends[piece + 1])
        held = {r: (parts[r][cut] + parts[r + 1][cut].astype(F32)).astype(BF16) for r in evens}
        sent = []
        bit = n_dp // 2
        while bit > 1:
            for r in [r for r in held if r & bit]:
                value = exchange(held.pop(r), bit)
                if r == bit:
                    sent.append(value)
                else:
                    held[r ^ bit] = held[r ^ bit] + value
            bit //= 2
        return sent

    ahead, behind, acts = add_and_send(half - 1, ahead, behind, acts, halves=True)
    down_sum = sum_step(down_sum, 0)
    parts = {}
    for r in evens:
        parts[r], parts[r + 1] = backward(r, 2, acts)
    ahead, behind, parts, down_sum, acts = fence(ahead, behind, parts, down_sum, acts)
    for r in evens:
        parts[r + 1] = exchange(parts[r + 1], 1)
    ahead, behind, acts = add_and_send(half - 2, ahead, behind, acts)
    down_sum = sum_step(down_sum, 1)
    parts, acts = fence(parts, acts)
    arriving = [partial_gradient(0)]
    (parts[1],) = backward(1, 1, acts)
    ahead, behind, parts, arriving, down_sum, acts = fence(
        ahead, behind, parts, arriving, down_sum, acts
    )
    for step in range(half - 3, 0, -1):
        ahead, behind, acts = add_and_send(step, ahead, behind, acts)
    arriving.append(partial_gradient(1))
    down_sum = sum_step(down_sum, 2)
    parts[1] = exchange(parts[1], 1)
    (parts[0],) = backward(0, 1, acts)
    ahead, behind, parts, arriving, down_sum, acts = fence(
        ahead, behind, parts, arriving, down_sum, acts
    )

    base_out = last_add(at, live_rows, total, ahead, behind, n_mp)
    base_out, parts, down_sum, acts = fence(base_out, parts, down_sum, acts)
    base_out = swap_places(base_out)
    branch, *terms = call(
        functools.partial(term_kernel, n_dp, owned),
        "term_up",
        [at, adapter_per_block, live_rows],
        [down_sum, masked_grad, block_up],
        [like((rows, width), F32)] + [like((rank, width), BF16)] * n_dp,
    )
    terms = [exchange(terms[r], r) if r else terms[0] for r in range(n_dp)]
    arriving.append(partial_gradient(2))
    hidden_gradient = blank((rows, units), BF16)
    for piece in range(2):
        hidden_gradient = combine(
            ends[piece], parts[0], parts[1], arriving[piece], hidden_gradient
        )
    groups = [hidden_0, near]
    for r in evens:
        groups += [piece[r] for piece in fetched] + [piece[r + 1] for piece in passed]
    down_grad = factor_grad(masks, acts, groups)
    down_grad = jnp.transpose(down_grad.reshape(owned, rank, units), (0, 2, 1))
    base_out, terms, arriving[2], hidden_gradient, down_grad, branch = fence(
        base_out, terms, arriving[2], hidden_gradient, down_grad, branch
    )
    (up_grad,) = call(
        functools.partial(up_grad_kernel, n_dp, blocks),
        "up_grad",
        [at, adapter_per_block],
        terms,
        [like((owned, rank, width), BF16)],
    )
    hidden_gradient = combine(ends[2], parts[0], parts[1], arriving[2], hidden_gradient)
    layer_out = (base_out.astype(F32) + branch).astype(BF16)
    return layer_out, hidden_gradient, down_grad, up_grad


def solution(mesh):
    return jax.shard_map(
        shards,
        mesh=mesh,
        in_specs=(
            P("dp", "mp"),
            P("mp", "dp"),
            P("dp", "mp", None),
            P("dp", None, "mp"),
            P("dp", "mp"),
            P(),
            P(),
        ),
        out_specs=(P("dp", "mp"), P("dp", "mp"), P("dp", "mp", None), P("dp", None, "mp")),
        check_vma=False,
    )
```

```python
import functools

import jax
import jax.numpy as jnp
from jax import lax
from jax.experimental import pallas as pl
from jax.experimental.pallas import tpu as pltpu
from jax.sharding import PartitionSpec as P

BLK = 128
SCALE = 8
F32 = jnp.float32
BF16 = jnp.bfloat16
VMEM_LIMIT = 44 * 1024 * 1024


TURNED = (((1,), (1,)), ((), ()))
FIRSTS = (((0,), (0,)), ((), ()))


def params():
    return pltpu.CompilerParams(vmem_limit_bytes=VMEM_LIMIT)


def cost(flops):
    return pl.CostEstimate(flops=int(flops), bytes_accessed=0, transcendentals=0)


def whole(shape):
    return pl.BlockSpec(shape, lambda *_: (0,) * len(shape))


def call(kernel, name, scalars, operands, out_shapes, scratch_shapes=()):
    return pl.pallas_call(
        kernel,
        grid_spec=pltpu.PrefetchScalarGridSpec(
            num_scalar_prefetch=len(scalars),
            grid=(1,),
            in_specs=[whole(x.shape) for x in operands],
            out_specs=[whole(x.shape) for x in out_shapes],
            scratch_shapes=list(scratch_shapes),
        ),
        out_shape=list(out_shapes),
        compiler_params=params(),
        name=name,
    )(*scalars, *operands)


def mask_kernel(at_ref, live_ref, grad_ref, out_ref):
    row = lax.broadcasted_iota(jnp.int32, grad_ref.shape, 0)
    grad = grad_ref[...]
    out_ref[...] = jnp.where(row < live_ref[at_ref[0]], grad, jnp.zeros_like(grad))


def select_kernel(n_dp, owned, rank, at_ref, id_ref, up_ref, *out_refs):
    mask_ref = out_refs[-1]
    dp = at_ref[0]
    blocks = mask_ref.shape[1]
    column = lax.broadcasted_iota(jnp.int32, (BLK, owned * rank), 1)
    for r in range(n_dp):
        chosen = jnp.int32(0)
        for b in range(blocks):
            local = id_ref[(dp ^ r) * blocks + b] - dp * owned
            chosen = jnp.where((local >= 0) & (local < owned), local, chosen)
            hit = (column >= local * rank) & (column < (local + 1) * rank)
            mask_ref[r, b] = jnp.where(hit, 1.0, 0.0).astype(BF16)
        out_refs[r][...] = up_ref[chosen]


def up_kernel(n_dp, owned, at_ref, id_ref, grad_ref, *refs):
    part_ref, block_ref = refs[n_dp:]
    dp = at_ref[0]
    blocks, rank, _ = block_ref.shape
    for b in range(blocks):
        source = (id_ref[dp * blocks + b] // owned) ^ dp
        for r in range(n_dp):

            @pl.when(source == r)
            def _():
                block_ref[b] = refs[r][...]

    for b in range(blocks):
        part_ref[b * rank : (b + 1) * rank, :] = lax.dot_general(
            block_ref[b],
            grad_ref[b * BLK : (b + 1) * BLK, :],
            TURNED,
            preferred_element_type=F32,
        )


def term_kernel(
    n_dp, owned, at_ref, id_ref, live_ref, down_ref, grad_ref, block_ref, branch_ref, *out_refs
):
    dp = at_ref[0]
    blocks, rank, width = block_ref.shape
    down_act = down_ref[...].astype(BF16)
    row = lax.broadcasted_iota(jnp.int32, (BLK, width), 0)
    for r in range(n_dp):
        out_refs[r][...] = jnp.zeros(out_refs[r].shape, BF16)
    for b in range(blocks):
        rows = slice(b * BLK, (b + 1) * BLK)
        act = down_act[b * rank : (b + 1) * rank]
        branch = lax.dot_general(act, block_ref[b], FIRSTS, preferred_element_type=F32)
        branch_ref[rows, :] = jnp.where(row + b * BLK < live_ref[dp], branch, 0.0)
        term = jnp.dot(act, grad_ref[rows, :], preferred_element_type=F32).astype(BF16)
        owner = (id_ref[dp * blocks + b] // owned) ^ dp
        for r in range(n_dp):

            @pl.when(owner == r)
            def _():
                out_refs[r][...] = term


def up_grad_kernel(n_dp, blocks, at_ref, id_ref, *refs):
    out_ref = refs[n_dp]
    dp = at_ref[0]
    owned = out_ref.shape[0]
    for a in range(owned):
        total = jnp.zeros(out_ref.shape[1:], F32)
        for r in range(n_dp):
            uses = jnp.int32(0)
            for b in range(blocks):
                uses += (id_ref[(dp ^ r) * blocks + b] == dp * owned + a).astype(jnp.int32)
            total += jnp.where(uses > 0, refs[r][...].astype(F32), 0.0)
        out_ref[a] = total.astype(BF16)


def ring_slot(offset, at, n_dp, n_mp):
    dp, mp = at[0], at[1]
    place = jnp.where(mp % 2 == 0, mp // 2, n_mp - 1 - mp // 2)
    there = (place + offset + n_mp) % n_mp
    index = jnp.where(there < n_mp // 2, 2 * there, 2 * (n_mp - 1 - there) + 1)
    q = n_mp // n_dp
    return (index // q) ^ dp, index % q


def add_kernel(at_ref, a_ref, b_ref, ahead_ref, behind_ref, a_out, b_out):
    a_out[...] = (a_ref[0, 0].astype(F32) + ahead_ref[...].astype(F32)).astype(BF16)
    b_out[...] = (b_ref[0, 0].astype(F32) + behind_ref[...].astype(F32)).astype(BF16)


def half_add_kernel(at_ref, a_ref, b_ref, ahead_ref, behind_ref, a_out, b_out):
    first = pl.program_id(0) == 0

    @pl.when(first)
    def _():
        a_out[...] = (a_ref[0, 0].astype(F32) + ahead_ref[...].astype(F32)).astype(BF16)
        b_out[...] = b_ref[0, 0]

    @pl.when(jnp.logical_not(first))
    def _():
        a_out[...] = a_ref[0, 0]
        b_out[...] = (b_ref[0, 0].astype(F32) + behind_ref[...].astype(F32)).astype(BF16)


def ring_add(step, at, total, ahead, behind, n_mp, halves):
    n_dp, _, rows, width = total.shape
    top = rows // 2

    def slot(offset):
        def index(i, at_ref):
            group, part = ring_slot(offset, at_ref, n_dp, n_mp)
            return group, part, i, 0

        return pl.BlockSpec((1, 1, top, width), index)

    arrived = pl.BlockSpec((top, width), lambda i, at_ref: (0 if halves else i, 0))
    sent = pl.BlockSpec((top, width), lambda i, at_ref: (i, 0))
    return pl.pallas_call(
        half_add_kernel if halves else add_kernel,
        grid_spec=pltpu.PrefetchScalarGridSpec(
            num_scalar_prefetch=1,
            grid=(2,),
            in_specs=[slot(step), slot(-step), arrived, arrived],
            out_specs=[sent, sent],
        ),
        out_shape=[jax.ShapeDtypeStruct((rows, width), BF16)] * 2,
        compiler_params=params(),
        name="ring_add",
    )(at, total, total, ahead, behind)


def opposite_kernel(at_ref, total_ref, first_ref, second_ref):
    top = first_ref.shape[0]
    first_ref[...] = total_ref[0, 0, :top]
    second_ref[...] = total_ref[0, 0, top:]


def opposite(at, total, n_mp):
    n_dp, _, rows, width = total.shape

    def index(i, at_ref):
        group, part = ring_slot(n_mp // 2, at_ref, n_dp, n_mp)
        return group, part, 0, 0

    out = pl.BlockSpec((rows // 2, width), lambda i, at_ref: (0, 0))
    return pl.pallas_call(
        opposite_kernel,
        grid_spec=pltpu.PrefetchScalarGridSpec(
            num_scalar_prefetch=1,
            grid=(1,),
            in_specs=[pl.BlockSpec((1, 1, rows, width), index)],
            out_specs=[out, out],
        ),
        out_shape=[jax.ShapeDtypeStruct((rows // 2, width), BF16)] * 2,
        compiler_params=params(),
        name="opposite",
    )(at, total)


def last_add_kernel(n_dp, n_mp, at_ref, live_ref, own_ref, ahead_ref, behind_ref, out_ref):
    total = own_ref[0, 0].astype(F32) + ahead_ref[...].astype(F32) + behind_ref[...].astype(F32)
    row = lax.broadcasted_iota(jnp.int32, total.shape, 0) + pl.program_id(0) * total.shape[0]
    live = live_ref[at_ref[1] // (n_mp // n_dp)]
    out_ref[...] = jnp.where(row < live, total, 0.0).astype(BF16)


def last_add(at, live_rows, total, ahead, behind, n_mp):
    n_dp, _, rows, width = total.shape

    def index(i, at_ref, live_ref):
        group, part = ring_slot(0, at_ref, n_dp, n_mp)
        return group, part, i, 0

    half = pl.BlockSpec((rows // 2, width), lambda i, at_ref, live_ref: (i, 0))
    return pl.pallas_call(
        functools.partial(last_add_kernel, n_dp, n_mp),
        grid_spec=pltpu.PrefetchScalarGridSpec(
            num_scalar_prefetch=2,
            grid=(2,),
            in_specs=[pl.BlockSpec((1, 1, rows // 2, width), index), half, half],
            out_specs=half,
        ),
        out_shape=jax.ShapeDtypeStruct((rows, width), BF16),
        compiler_params=params(),
        name="last_add",
    )(at, live_rows, total, ahead, behind)


def combine_kernel(own_ref, *refs):
    total = own_ref[...].astype(F32)
    for ref in refs[:-2]:
        total += ref[...].astype(F32)
    refs[-1][...] = total.astype(BF16)


def combine(start, own, near, arrived, out):
    rows, units = own.shape
    tile = 32
    first = start // tile
    placed = pl.BlockSpec((tile, units), lambda i: (i + first, 0))
    piece = pl.BlockSpec((tile, units), lambda i: (i, 0))
    return pl.pallas_call(
        combine_kernel,
        grid=(arrived[0].shape[0] // tile,),
        in_specs=[placed, placed]
        + [piece] * len(arrived)
        + [pl.BlockSpec(memory_space=pl.ANY)],
        out_specs=placed,
        out_shape=jax.ShapeDtypeStruct((rows, units), BF16),
        input_output_aliases={2 + len(arrived): 0},
        compiler_params=params(),
        name="combine",
    )(own, near, *arrived, out)


def blank_kernel(out_ref):
    pass


def blank(shape, dtype):
    return pl.pallas_call(
        blank_kernel,
        out_specs=pl.BlockSpec(memory_space=pl.ANY),
        out_shape=jax.ShapeDtypeStruct(shape, dtype),
        name="blank",
    )()


def forward_kernel(count, *refs):
    w_ref, a_ref, m_ref = refs[count : count + 3]
    y_ref, p_ref = refs[-2:]
    hid = jnp.concatenate([ref[...] for ref in refs[:count]], axis=0)
    out = jnp.dot(hid, w_ref[...], preferred_element_type=F32).astype(BF16)
    groups, _, blocks, _, tile = y_ref.shape
    y_ref[:, 0] = out.reshape(groups, blocks, BLK, tile)

    @pl.when(pl.program_id(0) == 0)
    def _():
        ranks = a_ref.shape[1]
        rank = p_ref.shape[1] // blocks
        part = jnp.dot(hid, a_ref[...], preferred_element_type=F32)
        part = jnp.where(m_ref[...].reshape(part.shape) > 0, part, 0.0)
        picked = part[:, :rank]
        for a in range(1, ranks // rank):
            picked = picked + part[:, a * rank : (a + 1) * rank]
        picked = picked.astype(BF16)
        row = lax.broadcasted_iota(jnp.int32, (BLK, BLK), 0)
        column = lax.broadcasted_iota(jnp.int32, (BLK, BLK), 1)
        unit = jnp.where(row == column, 1.0, 0.0).astype(BF16)
        for g in range(groups):
            for b in range(blocks):
                start = (g * blocks + b) * BLK
                p_ref[g, b * rank : (b + 1) * rank, :] = lax.dot_general(
                    picked[start : start + BLK], unit, FIRSTS, preferred_element_type=F32
                ).astype(BF16)


def forward_part(groups, blocks, hids, weight, factor, masks, total, q, rank):
    units, cols = weight.shape
    n_dp, all_blocks, _, ranks = masks.shape
    width = cols // q
    tile = min(512, width)
    per = width // tile
    group, block = groups[0] // groups[1], blocks[0] // blocks[1]
    in_specs = [whole(hid.shape) for hid in hids] + [
        pl.BlockSpec((units, tile), lambda i: (0, i)),
        whole((units, ranks)),
        pl.BlockSpec((groups[1], blocks[1], BLK, ranks), lambda i: (group, block, 0, 0)),
    ]
    operands = [*hids, weight, factor, masks]
    aliases = {}
    if total is not None:
        aliases = {len(operands): 0}
        in_specs.append(pl.BlockSpec(memory_space=pl.ANY))
        operands.append(total)
    turned = (groups[1], blocks[1] * rank, BLK)
    return pl.pallas_call(
        functools.partial(forward_kernel, len(hids)),
        grid=(cols // tile,),
        in_specs=in_specs,
        out_specs=[
            pl.BlockSpec(
                (groups[1], 1, blocks[1], BLK, tile),
                lambda i: (group, i // per, block, 0, i % per),
            ),
            whole(turned),
        ],
        out_shape=[
            jax.ShapeDtypeStruct((n_dp, q, all_blocks, BLK, width), BF16),
            jax.ShapeDtypeStruct(turned, BF16),
        ],
        input_output_aliases=aliases,
        cost_estimate=cost(SCALE * groups[1] * blocks[1] * BLK * units * cols),
        compiler_params=params(),
        name="forward_part",
    )(*operands)


def spread(act, mask):
    blocks, _, ranks = mask.shape
    rank = act.shape[0] // blocks
    row = lax.broadcasted_iota(jnp.int32, (rank, ranks), 0)
    column = lax.broadcasted_iota(jnp.int32, (rank, ranks), 1)
    repeat = jnp.where(column % rank == row, 1.0, 0.0).astype(BF16)
    wide = [
        lax.dot_general(
            act[b * rank : (b + 1) * rank], repeat, FIRSTS, preferred_element_type=F32
        )
        for b in range(blocks)
    ]
    wide = jnp.concatenate(wide, axis=0)
    return jnp.where(mask.reshape(wide.shape) > 0, wide, 0.0).astype(BF16)


def backward_kernel(groups, n_mp, offsets, at_ref, *refs):
    first, count = groups
    slots = len(offsets)
    block_refs = refs[: slots + 1]
    act_refs = refs[slots + 1 : slots + 1 + count]
    m_ref, w_ref, a_ref = refs[slots + 1 + count : slots + 4 + count]
    z_refs = refs[slots + 4 + count : -3]
    g_ref, u_ref, sems = refs[-3:]
    _, q, rows, _ = g_ref.shape
    n_dp = n_mp // q
    top = rows // 2

    def transfers(act):
        for index in range(slots + 1):
            there, part = ring_slot(offsets[min(index, slots - 1)], at_ref, n_dp, n_mp)
            target = g_ref.at[there % count, part]
            if index >= slots - 1:
                target = target.at[pl.ds(top * (index - slots + 1), top)]
            copy = pltpu.make_async_copy(block_refs[index], target, sems.at[index])
            pl.when(there // count == first // count)(copy.start if act else copy.wait)

    @pl.when(pl.program_id(0) == 0)
    def _():
        transfers(True)
        for g in range(count):
            u_ref[g * rows : (g + 1) * rows, :] = spread(act_refs[g][...], m_ref[g])
        transfers(False)

    grads = [
        jnp.concatenate([g_ref[g, h] for h in range(q)], axis=1) for g in range(count)
    ]
    out = lax.dot_general(
        jnp.concatenate(grads, axis=0), w_ref[...], TURNED, preferred_element_type=F32
    )
    out += jnp.dot(u_ref[...], a_ref[...], preferred_element_type=F32)
    for g in range(count):
        z_refs[g][...] = out[g * rows : (g + 1) * rows].astype(z_refs[g].dtype)


def backward_part(groups, at, blocks, offsets, acts, masks, weight, turned_factor, n_mp):
    units, cols = weight.shape
    n_dp, parts, _, ranks = masks.shape
    rows = parts * BLK
    q = n_mp // n_dp
    first, count = groups
    tile = min(896, units)
    return pl.pallas_call(
        functools.partial(backward_kernel, groups, n_mp, offsets),
        grid_spec=pltpu.PrefetchScalarGridSpec(
            num_scalar_prefetch=1,
            grid=(pl.cdiv(units, tile),),
            in_specs=[pl.BlockSpec(memory_space=pl.ANY)] * len(blocks)
            + [whole(act.shape) for act in acts]
            + [
                pl.BlockSpec(
                    (count, parts, BLK, ranks), lambda i, at_ref: (first // count, 0, 0, 0)
                ),
                pl.BlockSpec((tile, cols), lambda i, at_ref: (i, 0)),
                pl.BlockSpec((ranks, tile), lambda i, at_ref: (0, i)),
            ],
            out_specs=[pl.BlockSpec((rows, tile), lambda i, at_ref: (0, i))] * count,
            scratch_shapes=[
                pltpu.VMEM((count, q, rows, cols // q), BF16),
                pltpu.VMEM((count * rows, ranks), BF16),
                pltpu.SemaphoreType.DMA((len(blocks),)),
            ],
        ),
        out_shape=[
            jax.ShapeDtypeStruct((rows, units), BF16)
        ]
        * count,
        cost_estimate=cost(SCALE * count * rows * units * cols),
        compiler_params=params(),
        name="backward_part",
    )(at, *blocks, *acts, masks, weight, turned_factor)


def factor_grad_kernel(n_dp, m_ref, *refs):
    acts = [spread(refs[r][...], m_ref[r]) for r in range(n_dp)]
    hid = jnp.concatenate([ref[...] for ref in refs[n_dp:-1]], axis=0)
    out = lax.dot_general(
        jnp.concatenate(acts, axis=0), hid, FIRSTS, preferred_element_type=F32
    )
    refs[-1][...] = out.astype(BF16)


def factor_grad(masks, acts, hids):
    ranks = masks.shape[3]
    units = hids[0].shape[1]
    tile = units // 2 if units % 256 == 0 else units
    return pl.pallas_call(
        functools.partial(factor_grad_kernel, len(acts)),
        grid=(units // tile,),
        in_specs=[whole(masks.shape)]
        + [whole(act.shape) for act in acts]
        + [pl.BlockSpec((hid.shape[0], tile), lambda i: (0, i)) for hid in hids],
        out_specs=pl.BlockSpec((ranks, tile), lambda i: (0, i)),
        out_shape=jax.ShapeDtypeStruct((ranks, units), BF16),
        compiler_params=params(),
        name="factor_grad",
    )(masks, *acts, *hids)


def shards(
    hidden, down_weight, adapter_down, adapter_up, output_grad, adapter_per_block, live_rows
):
    n_dp = lax.axis_size("dp")
    n_mp = lax.axis_size("mp")
    at = jnp.stack([lax.axis_index("dp"), lax.axis_index("mp")])
    q = n_mp // n_dp
    rows, units = hidden.shape
    width = output_grad.shape[1]
    owned, _, rank = adapter_down.shape
    blocks = rows // BLK
    half = n_mp // 2
    top = rows // 2
    fence = lambda *values: lax.optimization_barrier(values)
    like = jax.ShapeDtypeStruct

    def exchange(value, bit, axis="dp"):
        count = n_dp if axis == "dp" else n_mp
        return lax.ppermute(value, axis, [(i, i ^ bit) for i in range(count)])

    def swap_places(value):
        pairs = [
            (j * n_mp + m, (m // q) * n_mp + j * q + m % q)
            for j in range(n_dp)
            for m in range(n_mp)
        ]
        return lax.ppermute(value, ("dp", "mp"), pairs)

    ring = list(range(0, n_mp, 2)) + list(range(n_mp - 1, 0, -2))
    up_ring = [(ring[i], ring[(i + 1) % n_mp]) for i in range(n_mp)]
    down_ring = [(b, a) for a, b in up_ring]

    def onward(value):
        return lax.ppermute(value, "mp", up_ring)

    def backward_on(value):
        return lax.ppermute(value, "mp", down_ring)

    evens = range(2, n_dp, 2)
    cuts = [0, rows // 4, 2 * rows // 3, rows]

    def fetch(hidden, piece):
        held = {0: hidden[cuts[piece] : cuts[piece + 1]]}
        bit = 2
        while bit < n_dp:
            for r in list(held):
                held[r ^ bit] = exchange(held[r], bit)
            bit *= 2
        return {r: held[r] for r in evens}

    def pass_on(fetched):
        return {r + 1: exchange(fetched[r], 1) for r in evens}

    far_steps = [1 << k for k in range(n_mp.bit_length() - 2, -1, -1)]
    sum_steps = [far_steps[:-2], far_steps[-2:-1], far_steps[-1:]]

    def sum_step(value, index):
        for bit in sum_steps[index]:
            value = value + exchange(value.astype(BF16), bit, "mp").astype(F32)
        return value

    (masked_grad,) = call(
        mask_kernel, "mask", [at, live_rows], [output_grad], [like(output_grad.shape, BF16)]
    )
    swapped = swap_places(masked_grad)
    near = exchange(hidden, 1)
    adapter_up, masked_grad, at = fence(adapter_up, masked_grad, at)
    *chosen, masks = call(
        functools.partial(select_kernel, n_dp, owned, rank),
        "select",
        [at, adapter_per_block],
        [adapter_up],
        [like((rank, width), BF16)] * n_dp + [like((n_dp, blocks, BLK, owned * rank), BF16)],
    )
    arrived_up = [exchange(chosen[r], r) if r else chosen[0] for r in range(n_dp)]
    arrived_up[1], hidden_0 = fence(arrived_up[1], hidden)
    fetched = [fetch(hidden_0, 0)]
    turned_factor = jnp.transpose(adapter_down, (0, 2, 1)).reshape(owned * rank, units)
    factor = turned_factor.T

    def forward(groups, span, hids, total):
        return forward_part(groups, span, hids, down_weight, factor, masks, total, q, rank)

    picked = {}
    total, own = forward((0, 1), (0, blocks), [hidden], None)
    picked[0] = [own[0]]
    arrived_up, total, hidden = fence(arrived_up, total, hidden)
    up_sum, block_up = call(
        functools.partial(up_kernel, n_dp, owned),
        "up_part",
        [at, adapter_per_block],
        [masked_grad, *arrived_up],
        [like((blocks * rank, BLK), F32), like((blocks, rank, width), BF16)],
    )
    up_sum = sum_step(up_sum, 0)
    swapped, near, fetched[0], total, up_sum, hidden = fence(
        swapped, near, fetched[0], total, up_sum, hidden
    )

    ahead = behind = swapped
    ring_blocks = [swapped]
    offsets = [0] + [sign * step for step in range(1, half) for sign in (-1, 1)] + [half]
    ahead, behind = onward(ahead), backward_on(behind)
    fetched.append(fetch(hidden, 1))
    passed = [pass_on(fetched[0])]
    up_sum = sum_step(up_sum, 1)
    total, own = forward((1, 1), (0, blocks), [near], total)
    picked[1] = [own[0]]
    ahead, behind, fetched[1], passed, total, up_sum, hidden = fence(
        ahead, behind, fetched[1], passed, total, up_sum, hidden
    )
    ring_blocks += [ahead, behind]
    ahead, behind = onward(ahead), backward_on(behind)
    fetched.append(fetch(hidden, 2))
    passed.append(pass_on(fetched[1]))

    def forward_pairs(span, pieces, total):
        for r in evens:
            hids = [fetched[p][r] for p in pieces] + [passed[p][r + 1] for p in pieces]
            total, pair = forward((r, 2), span, hids, total)
            for g in range(2):
                picked.setdefault(r + g, []).append(pair[g])
        return total

    total = forward_pairs((0, 2), (0, 1), total)
    total, up_sum = fence(total, up_sum)
    up_sum = sum_step(up_sum, 2)
    ahead, behind, fetched[2], passed, total, up_sum = fence(
        ahead, behind, fetched[2], passed, total, up_sum
    )
    ring_blocks += [ahead, behind]
    for _ in range(3, half):
        ahead, behind = onward(ahead), backward_on(behind)
        ring_blocks += [ahead, behind]
    passed.append(pass_on(fetched[2]))
    passed, up_act = fence(passed, up_sum.astype(BF16))
    acts = [exchange(up_act, r) if r else up_act for r in range(n_dp)]
    total = forward_pairs((2, 1), (2,), total)
    ahead, behind, acts, total, picked = fence(ahead, behind, acts, total, picked)
    ring_blocks[-2:] = [ahead, behind]
    total = total.reshape(n_dp, q, rows, width)

    last = [onward(ahead[:top]), backward_on(behind[top:])]
    ahead, behind = opposite(at, total, n_mp)
    ahead, behind = onward(ahead), backward_on(behind)
    held = {r: jnp.concatenate(picked[r], axis=0) for r in range(n_dp)}
    bit = 1
    while bit < n_dp:
        sent = [r for r in held if r & bit]
        arrived = exchange(jnp.concatenate([held.pop(r).astype(BF16) for r in sent]), bit)
        for index, r in enumerate(sent):
            size = blocks * rank
            piece = arrived[index * size : (index + 1) * size]
            held[r ^ bit] = held[r ^ bit].astype(F32) + piece.astype(F32)
        bit *= 2
    down_sum = held[0]
    last, ahead, behind, down_sum, acts = fence(last, ahead, behind, down_sum, acts)
    ring_blocks += last

    def backward(first, count, acts):
        return backward_part(
            (first, count),
            at,
            ring_blocks,
            offsets,
            acts[first : first + count],
            masks,
            down_weight,
            turned_factor,
            n_mp,
        )

    def add_and_send(step, ahead, behind, *others, halves=False):
        ahead, behind = ring_add(step, at, total, ahead, behind, n_mp, halves)
        ahead, behind, *others = fence(ahead, behind, *others)
        return onward(ahead), backward_on(behind), *others

    ends = [0, rows // 3, 3 * rows // 4, rows]

    def partial_gradient(piece):
        cut = slice(ends[piece], ends[piece + 1])
        held = {
            r: (parts[r][cut].astype(F32) + parts[r + 1][cut].astype(F32)).astype(BF16)
            for r in evens
        }
        sent = []
        bit = n_dp // 2
        while bit > 1:
            for r in [r for r in held if r & bit]:
                value = exchange(held.pop(r), bit)
                if r == bit:
                    sent.append(value)
                else:
                    held[r ^ bit] = held[r ^ bit] + value
            bit //= 2
        return sent

    ahead, behind, acts = add_and_send(half - 1, ahead, behind, acts, halves=True)
    down_sum = sum_step(down_sum, 0)
    parts = {}
    for r in evens:
        parts[r], parts[r + 1] = backward(r, 2, acts)
    ahead, behind, parts, down_sum, acts = fence(ahead, behind, parts, down_sum, acts)
    ahead, behind, acts, parts = add_and_send(half - 2, ahead, behind, acts, parts)
    for r in evens:
        parts[r + 1] = exchange(parts[r + 1], 1)
    parts, acts = fence(parts, acts)
    arriving = [partial_gradient(0)]
    (parts[1],) = backward(1, 1, acts)
    parts[1], down_sum = fence(parts[1], down_sum)
    down_sum = sum_step(down_sum, 1)
    ahead, behind, parts, arriving, down_sum, acts = fence(
        ahead, behind, parts, arriving, down_sum, acts
    )
    for step in range(half - 3, 0, -1):
        ahead, behind, acts, parts = add_and_send(step, ahead, behind, acts, parts)
    arriving.append(partial_gradient(1))
    down_sum = sum_step(down_sum, 2)
    parts[1] = exchange(parts[1], 1)
    (parts[0],) = backward(0, 1, acts)
    ahead, behind, parts, arriving, down_sum, acts = fence(
        ahead, behind, parts, arriving, down_sum, acts
    )

    base_out = last_add(at, live_rows, total, ahead, behind, n_mp)
    branch, *terms = call(
        functools.partial(term_kernel, n_dp, owned),
        "term_up",
        [at, adapter_per_block, live_rows],
        [down_sum, masked_grad, block_up],
        [like((rows, width), F32)] + [like((rank, width), BF16)] * n_dp,
    )
    base_out, terms, parts, acts = fence(base_out, terms, parts, acts)
    base_out = swap_places(base_out)
    terms = [exchange(terms[r], r) if r else terms[0] for r in range(n_dp)]
    arriving.append(partial_gradient(2))
    hidden_gradient = blank((rows, units), BF16)
    for piece in range(2):
        hidden_gradient = combine(
            ends[piece], parts[0], parts[1], arriving[piece], hidden_gradient
        )
    groups = [hidden_0, near]
    for r in evens:
        groups += [piece[r] for piece in fetched] + [piece[r + 1] for piece in passed]
    down_grad = factor_grad(masks, acts, groups)
    down_grad = jnp.transpose(down_grad.reshape(owned, rank, units), (0, 2, 1))
    base_out, terms, hidden_gradient, down_grad, branch = fence(
        base_out, terms, hidden_gradient, down_grad, branch
    )
    (up_grad,) = call(
        functools.partial(up_grad_kernel, n_dp, blocks),
        "up_grad",
        [at, adapter_per_block],
        terms,
        [like((owned, rank, width), BF16)],
    )
    layer_out = (base_out.astype(F32) + branch).astype(BF16)
    layer_out, up_grad, arriving[2] = fence(layer_out, up_grad, arriving[2])
    hidden_gradient = combine(ends[2], parts[0], parts[1], arriving[2], hidden_gradient)
    return layer_out, hidden_gradient, down_grad, up_grad


def solution(mesh):
    return jax.shard_map(
        shards,
        mesh=mesh,
        in_specs=(
            P("dp", "mp"),
            P("mp", "dp"),
            P("dp", "mp", None),
            P("dp", None, "mp"),
            P("dp", "mp"),
            P(),
            P(),
        ),
        out_specs=(P("dp", "mp"), P("dp", "mp"), P("dp", "mp", None), P("dp", None, "mp")),
        check_vma=False,
    )
```

```python
import functools

import jax
import jax.numpy as jnp
from jax import lax
from jax.experimental import pallas as pl
from jax.experimental.pallas import tpu as pltpu
from jax.sharding import PartitionSpec as P

BLK = 128
LOW, HIGH = 2, 8
F32 = jnp.float32
BF16 = jnp.bfloat16
VMEM_LIMIT = 44 * 1024 * 1024


TURNED = (((1,), (1,)), ((), ()))
FIRSTS = (((0,), (0,)), ((), ()))


def params():
    return pltpu.CompilerParams(vmem_limit_bytes=VMEM_LIMIT)


def cost(flops):
    return pl.CostEstimate(flops=int(flops), bytes_accessed=0, transcendentals=0)


def whole(shape):
    return pl.BlockSpec(shape, lambda *_: (0,) * len(shape))


def call(kernel, name, scalars, operands, out_shapes, scratch_shapes=()):
    return pl.pallas_call(
        kernel,
        grid_spec=pltpu.PrefetchScalarGridSpec(
            num_scalar_prefetch=len(scalars),
            grid=(1,),
            in_specs=[whole(x.shape) for x in operands],
            out_specs=[whole(x.shape) for x in out_shapes],
            scratch_shapes=list(scratch_shapes),
        ),
        out_shape=list(out_shapes),
        compiler_params=params(),
        name=name,
    )(*scalars, *operands)


def mask_kernel(at_ref, live_ref, grad_ref, out_ref):
    row = lax.broadcasted_iota(jnp.int32, grad_ref.shape, 0)
    grad = grad_ref[...]
    out_ref[...] = jnp.where(row < live_ref[at_ref[0]], grad, jnp.zeros_like(grad))


def select_kernel(n_dp, owned, rank, at_ref, id_ref, up_ref, *out_refs):
    mask_ref = out_refs[-1]
    dp = at_ref[0]
    blocks = mask_ref.shape[1]
    column = lax.broadcasted_iota(jnp.int32, (BLK, owned * rank), 1)
    for r in range(n_dp):
        chosen = jnp.int32(0)
        for b in range(blocks):
            local = id_ref[(dp ^ r) * blocks + b] - dp * owned
            chosen = jnp.where((local >= 0) & (local < owned), local, chosen)
            hit = (column >= local * rank) & (column < (local + 1) * rank)
            mask_ref[r, b] = jnp.where(hit, 1.0, 0.0).astype(BF16)
        out_refs[r][...] = up_ref[chosen]


def up_kernel(n_dp, owned, at_ref, id_ref, grad_ref, *refs):
    part_ref, block_ref = refs[n_dp:]
    dp = at_ref[0]
    blocks, rank, _ = block_ref.shape
    for b in range(blocks):
        source = (id_ref[dp * blocks + b] // owned) ^ dp
        for r in range(n_dp):

            @pl.when(source == r)
            def _():
                block_ref[b] = refs[r][...]

    for b in range(blocks):
        part_ref[b * rank : (b + 1) * rank, :] = lax.dot_general(
            block_ref[b],
            grad_ref[b * BLK : (b + 1) * BLK, :],
            TURNED,
            preferred_element_type=F32,
        )


def term_kernel(
    n_dp, owned, at_ref, id_ref, live_ref, down_ref, grad_ref, block_ref, branch_ref, *out_refs
):
    dp = at_ref[0]
    blocks, rank, width = block_ref.shape
    down_act = down_ref[...].astype(BF16)
    row = lax.broadcasted_iota(jnp.int32, (BLK, width), 0)
    for r in range(n_dp):
        out_refs[r][...] = jnp.zeros(out_refs[r].shape, BF16)
    for b in range(blocks):
        rows = slice(b * BLK, (b + 1) * BLK)
        act = down_act[b * rank : (b + 1) * rank]
        branch = lax.dot_general(act, block_ref[b], FIRSTS, preferred_element_type=F32)
        branch_ref[rows, :] = jnp.where(row + b * BLK < live_ref[dp], branch, 0.0)
        term = jnp.dot(act, grad_ref[rows, :], preferred_element_type=F32).astype(BF16)
        owner = (id_ref[dp * blocks + b] // owned) ^ dp
        for r in range(n_dp):

            @pl.when(owner == r)
            def _():
                out_refs[r][...] = term


def up_grad_kernel(n_dp, blocks, at_ref, id_ref, *refs):
    out_ref = refs[n_dp]
    dp = at_ref[0]
    owned = out_ref.shape[0]
    for a in range(owned):
        total = jnp.zeros(out_ref.shape[1:], F32)
        for r in range(n_dp):
            uses = jnp.int32(0)
            for b in range(blocks):
                uses += (id_ref[(dp ^ r) * blocks + b] == dp * owned + a).astype(jnp.int32)
            total += jnp.where(uses > 0, refs[r][...].astype(F32), 0.0)
        out_ref[a] = total.astype(BF16)


def ring_slot(offset, at, n_dp, n_mp):
    dp, mp = at[0], at[1]
    place = jnp.where(mp % 2 == 0, mp // 2, n_mp - 1 - mp // 2)
    there = (place + offset + n_mp) % n_mp
    index = jnp.where(there < n_mp // 2, 2 * there, 2 * (n_mp - 1 - there) + 1)
    q = n_mp // n_dp
    return (index // q) ^ dp, index % q


def add_kernel(at_ref, a_ref, b_ref, ahead_ref, behind_ref, a_out, b_out):
    a_out[...] = (a_ref[0, 0].astype(F32) + ahead_ref[...].astype(F32)).astype(BF16)
    b_out[...] = (b_ref[0, 0].astype(F32) + behind_ref[...].astype(F32)).astype(BF16)


def half_add_kernel(at_ref, a_ref, b_ref, ahead_ref, behind_ref, a_out, b_out):
    first = pl.program_id(0) == 0

    @pl.when(first)
    def _():
        a_out[...] = (a_ref[0, 0].astype(F32) + ahead_ref[...].astype(F32)).astype(BF16)
        b_out[...] = b_ref[0, 0]

    @pl.when(jnp.logical_not(first))
    def _():
        a_out[...] = a_ref[0, 0]
        b_out[...] = (b_ref[0, 0].astype(F32) + behind_ref[...].astype(F32)).astype(BF16)


def ring_add(step, at, total, ahead, behind, n_mp, halves):
    n_dp, _, rows, width = total.shape
    top = rows // 2

    def slot(offset):
        def index(i, at_ref):
            group, part = ring_slot(offset, at_ref, n_dp, n_mp)
            return group, part, i, 0

        return pl.BlockSpec((1, 1, top, width), index)

    arrived = pl.BlockSpec((top, width), lambda i, at_ref: (0 if halves else i, 0))
    sent = pl.BlockSpec((top, width), lambda i, at_ref: (i, 0))
    return pl.pallas_call(
        half_add_kernel if halves else add_kernel,
        grid_spec=pltpu.PrefetchScalarGridSpec(
            num_scalar_prefetch=1,
            grid=(2,),
            in_specs=[slot(step), slot(-step), arrived, arrived],
            out_specs=[sent, sent],
        ),
        out_shape=[jax.ShapeDtypeStruct((rows, width), BF16)] * 2,
        compiler_params=params(),
        name="ring_add",
    )(at, total, total, ahead, behind)


def opposite_kernel(at_ref, total_ref, first_ref, second_ref):
    top = first_ref.shape[0]
    first_ref[...] = total_ref[0, 0, :top]
    second_ref[...] = total_ref[0, 0, top:]


def opposite(at, total, n_mp):
    n_dp, _, rows, width = total.shape

    def index(i, at_ref):
        group, part = ring_slot(n_mp // 2, at_ref, n_dp, n_mp)
        return group, part, 0, 0

    out = pl.BlockSpec((rows // 2, width), lambda i, at_ref: (0, 0))
    return pl.pallas_call(
        opposite_kernel,
        grid_spec=pltpu.PrefetchScalarGridSpec(
            num_scalar_prefetch=1,
            grid=(1,),
            in_specs=[pl.BlockSpec((1, 1, rows, width), index)],
            out_specs=[out, out],
        ),
        out_shape=[jax.ShapeDtypeStruct((rows // 2, width), BF16)] * 2,
        compiler_params=params(),
        name="opposite",
    )(at, total)


def last_add_kernel(n_dp, n_mp, at_ref, live_ref, own_ref, ahead_ref, behind_ref, out_ref):
    total = own_ref[0, 0].astype(F32) + ahead_ref[...].astype(F32) + behind_ref[...].astype(F32)
    row = lax.broadcasted_iota(jnp.int32, total.shape, 0) + pl.program_id(0) * total.shape[0]
    live = live_ref[at_ref[1] // (n_mp // n_dp)]
    out_ref[...] = jnp.where(row < live, total, 0.0).astype(BF16)


def last_add(at, live_rows, total, ahead, behind, n_mp):
    n_dp, _, rows, width = total.shape

    def index(i, at_ref, live_ref):
        group, part = ring_slot(0, at_ref, n_dp, n_mp)
        return group, part, i, 0

    half = pl.BlockSpec((rows // 2, width), lambda i, at_ref, live_ref: (i, 0))
    return pl.pallas_call(
        functools.partial(last_add_kernel, n_dp, n_mp),
        grid_spec=pltpu.PrefetchScalarGridSpec(
            num_scalar_prefetch=2,
            grid=(2,),
            in_specs=[pl.BlockSpec((1, 1, rows // 2, width), index), half, half],
            out_specs=half,
        ),
        out_shape=jax.ShapeDtypeStruct((rows, width), BF16),
        compiler_params=params(),
        name="last_add",
    )(at, live_rows, total, ahead, behind)


def combine_kernel(own_ref, *refs):
    total = own_ref[...].astype(F32)
    for ref in refs[:-2]:
        total += ref[...].astype(F32)
    refs[-1][...] = total.astype(BF16)


def combine(start, own, near, arrived, out):
    rows, units = own.shape
    tile = 48
    first = start // tile
    placed = pl.BlockSpec((tile, units), lambda i: (i + first, 0))
    piece = pl.BlockSpec((tile, units), lambda i: (i, 0))
    return pl.pallas_call(
        combine_kernel,
        grid=(arrived[0].shape[0] // tile,),
        in_specs=[placed, placed]
        + [piece] * len(arrived)
        + [pl.BlockSpec(memory_space=pl.ANY)],
        out_specs=placed,
        out_shape=jax.ShapeDtypeStruct((rows, units), BF16),
        input_output_aliases={2 + len(arrived): 0},
        compiler_params=params(),
        name="combine",
    )(own, near, *arrived, out)


def blank_kernel(out_ref):
    pass


def blank(shape, dtype):
    return pl.pallas_call(
        blank_kernel,
        out_specs=pl.BlockSpec(memory_space=pl.ANY),
        out_shape=jax.ShapeDtypeStruct(shape, dtype),
        name="blank",
    )()


def forward_kernel(count, *refs):
    w_ref, a_ref, m_ref = refs[count : count + 3]
    y_ref, p_ref = refs[-2:]
    hid = jnp.concatenate([ref[...] for ref in refs[:count]], axis=0)
    out = jnp.dot(hid, w_ref[...], preferred_element_type=F32).astype(BF16)
    groups, _, blocks, _, tile = y_ref.shape
    y_ref[:, 0] = out.reshape(groups, blocks, BLK, tile)

    @pl.when(pl.program_id(0) == 0)
    def _():
        ranks = a_ref.shape[1]
        rank = p_ref.shape[1] // blocks
        part = jnp.dot(hid, a_ref[...], preferred_element_type=F32)
        part = jnp.where(m_ref[...].reshape(part.shape) > 0, part, 0.0)
        picked = part[:, :rank]
        for a in range(1, ranks // rank):
            picked = picked + part[:, a * rank : (a + 1) * rank]
        picked = picked.astype(BF16)
        row = lax.broadcasted_iota(jnp.int32, (BLK, BLK), 0)
        column = lax.broadcasted_iota(jnp.int32, (BLK, BLK), 1)
        unit = jnp.where(row == column, 1.0, 0.0).astype(BF16)
        for g in range(groups):
            for b in range(blocks):
                start = (g * blocks + b) * BLK
                p_ref[g, b * rank : (b + 1) * rank, :] = lax.dot_general(
                    picked[start : start + BLK], unit, FIRSTS, preferred_element_type=F32
                ).astype(BF16)


def forward_part(groups, blocks, hids, weight, factor, masks, total, q, rank):
    units, cols = weight.shape
    n_dp, all_blocks, _, ranks = masks.shape
    width = cols // q
    tile = min(512, width)
    per = width // tile
    group, block = groups[0] // groups[1], blocks[0] // blocks[1]
    in_specs = [whole(hid.shape) for hid in hids] + [
        pl.BlockSpec((units, tile), lambda i: (0, i)),
        whole((units, ranks)),
        pl.BlockSpec((groups[1], blocks[1], BLK, ranks), lambda i: (group, block, 0, 0)),
    ]
    operands = [*hids, weight, factor, masks]
    aliases = {}
    if total is not None:
        aliases = {len(operands): 0}
        in_specs.append(pl.BlockSpec(memory_space=pl.ANY))
        operands.append(total)
    turned = (groups[1], blocks[1] * rank, BLK)
    return pl.pallas_call(
        functools.partial(forward_kernel, len(hids)),
        grid=(cols // tile,),
        in_specs=in_specs,
        out_specs=[
            pl.BlockSpec(
                (groups[1], 1, blocks[1], BLK, tile),
                lambda i: (group, i // per, block, 0, i % per),
            ),
            whole(turned),
        ],
        out_shape=[
            jax.ShapeDtypeStruct((n_dp, q, all_blocks, BLK, width), BF16),
            jax.ShapeDtypeStruct(turned, BF16),
        ],
        input_output_aliases=aliases,
        cost_estimate=cost(LOW * groups[1] * blocks[1] * BLK * units * cols),
        compiler_params=params(),
        name="forward_part",
    )(*operands)


def spread(act, mask):
    blocks, _, ranks = mask.shape
    rank = act.shape[0] // blocks
    row = lax.broadcasted_iota(jnp.int32, (rank, ranks), 0)
    column = lax.broadcasted_iota(jnp.int32, (rank, ranks), 1)
    repeat = jnp.where(column % rank == row, 1.0, 0.0).astype(BF16)
    wide = [
        lax.dot_general(
            act[b * rank : (b + 1) * rank], repeat, FIRSTS, preferred_element_type=F32
        )
        for b in range(blocks)
    ]
    wide = jnp.concatenate(wide, axis=0)
    return jnp.where(mask.reshape(wide.shape) > 0, wide, 0.0).astype(BF16)


def backward_kernel(group, n_mp, offsets, more, at_ref, *refs):
    slots = len(offsets)
    block_refs = refs[: slots + 1]
    act_ref, m_ref, w_ref, a_ref = refs[slots + 1 : slots + 5]
    z_refs = refs[slots + 5 + more : -3]
    g_ref, u_ref, sems = refs[-3:]
    q, rows, _ = g_ref.shape
    n_dp = n_mp // q
    top = rows // 2

    def transfers(act):
        for index in range(slots + 1):
            there, part = ring_slot(offsets[min(index, slots - 1)], at_ref, n_dp, n_mp)
            target = g_ref.at[part]
            if index >= slots - 1:
                target = target.at[pl.ds(top * (index - slots + 1), top)]
            copy = pltpu.make_async_copy(block_refs[index], target, sems.at[index])
            pl.when(there == group)(copy.start if act else copy.wait)

    @pl.when(pl.program_id(0) == 0)
    def _():
        transfers(True)
        u_ref[...] = spread(act_ref[...], m_ref[0])
        transfers(False)

    out = lax.dot_general(
        jnp.concatenate([g_ref[h] for h in range(q)], axis=1),
        w_ref[...],
        TURNED,
        preferred_element_type=F32,
    )
    out += jnp.dot(u_ref[...], a_ref[...], preferred_element_type=F32)
    for ref in refs[slots + 5 : slots + 5 + more]:
        out += ref[...].astype(F32)
    start = 0
    for z_ref in z_refs:
        size = z_ref.shape[0]
        z_ref[...] = out[start : start + size].astype(BF16)
        start += size


def backward_part(
    group, at, blocks, offsets, act, masks, weight, turned_factor, n_mp, others, pieces
):
    units, cols = weight.shape
    n_dp, parts, _, ranks = masks.shape
    rows = parts * BLK
    q = n_mp // n_dp
    tile = min(896, units)
    columns = lambda i, at_ref: (0, i)
    return pl.pallas_call(
        functools.partial(backward_kernel, group, n_mp, offsets, len(others)),
        grid_spec=pltpu.PrefetchScalarGridSpec(
            num_scalar_prefetch=1,
            grid=(pl.cdiv(units, tile),),
            in_specs=[pl.BlockSpec(memory_space=pl.ANY)] * len(blocks)
            + [
                whole(act.shape),
                pl.BlockSpec((1, parts, BLK, ranks), lambda i, at_ref: (group, 0, 0, 0)),
                pl.BlockSpec((tile, cols), lambda i, at_ref: (i, 0)),
                pl.BlockSpec((ranks, tile), columns),
            ]
            + [pl.BlockSpec((rows, tile), columns)] * len(others),
            out_specs=[pl.BlockSpec((size, tile), columns) for size in pieces],
            scratch_shapes=[
                pltpu.VMEM((q, rows, cols // q), BF16),
                pltpu.VMEM((rows, ranks), BF16),
                pltpu.SemaphoreType.DMA((len(blocks),)),
            ],
        ),
        out_shape=[jax.ShapeDtypeStruct((size, units), BF16) for size in pieces],
        cost_estimate=cost((HIGH if others else LOW) * rows * units * cols),
        compiler_params=params(),
        name="backward_part",
    )(at, *blocks, act, masks, weight, turned_factor, *others)


def factor_grad_kernel(n_dp, m_ref, *refs):
    acts = [spread(refs[r][...], m_ref[r]) for r in range(n_dp)]
    hid = jnp.concatenate([ref[...] for ref in refs[n_dp:-1]], axis=0)
    out = lax.dot_general(
        jnp.concatenate(acts, axis=0), hid, FIRSTS, preferred_element_type=F32
    )
    refs[-1][...] = out.astype(BF16)


def factor_grad(masks, acts, hids):
    ranks = masks.shape[3]
    units = hids[0].shape[1]
    tile = units // 2 if units % 256 == 0 else units
    return pl.pallas_call(
        functools.partial(factor_grad_kernel, len(acts)),
        grid=(units // tile,),
        in_specs=[whole(masks.shape)]
        + [whole(act.shape) for act in acts]
        + [pl.BlockSpec((hid.shape[0], tile), lambda i: (0, i)) for hid in hids],
        out_specs=pl.BlockSpec((ranks, tile), lambda i: (0, i)),
        out_shape=jax.ShapeDtypeStruct((ranks, units), BF16),
        compiler_params=params(),
        name="factor_grad",
    )(masks, *acts, *hids)


def shards(
    hidden, down_weight, adapter_down, adapter_up, output_grad, adapter_per_block, live_rows
):
    n_dp = lax.axis_size("dp")
    n_mp = lax.axis_size("mp")
    at = jnp.stack([lax.axis_index("dp"), lax.axis_index("mp")])
    q = n_mp // n_dp
    rows, units = hidden.shape
    width = output_grad.shape[1]
    owned, _, rank = adapter_down.shape
    blocks = rows // BLK
    half = n_mp // 2
    top = rows // 2
    fence = lambda *values: lax.optimization_barrier(values)
    like = jax.ShapeDtypeStruct

    def exchange(value, bit, axis="dp"):
        count = n_dp if axis == "dp" else n_mp
        return lax.ppermute(value, axis, [(i, i ^ bit) for i in range(count)])

    def swap_places(value):
        index = lambda j, m: j * n_mp + m
        near_pairs, far = [], []
        for j in range(n_dp):
            for m in range(n_mp):
                c, h = m // q, m % q
                if c // 2 == j // 2 or n_dp != 4:
                    near_pairs.append((index(j, m), index(c, j * q + h)))
                else:
                    far.append((j, c, h))
        swapped = lax.ppermute(value, ("dp", "mp"), near_pairs)
        if far:
            routes = (
                lambda j, c, h: index(j ^ 2, c * q + h),
                lambda j, c, h: index(c ^ 2, j * q + h),
            )
            halves = []
            for route, half_rows in zip(routes, (value[:top], value[top:])):
                first = [(index(j, c * q + h), route(j, c, h)) for j, c, h in far]
                second = [(route(j, c, h), index(c, j * q + h)) for j, c, h in far]
                halves.append(
                    lax.ppermute(
                        lax.ppermute(half_rows, ("dp", "mp"), first), ("dp", "mp"), second
                    )
                )
            swapped = swapped + jnp.concatenate(halves, axis=0)
        return swapped

    ring = list(range(0, n_mp, 2)) + list(range(n_mp - 1, 0, -2))
    up_ring = [(ring[i], ring[(i + 1) % n_mp]) for i in range(n_mp)]
    down_ring = [(b, a) for a, b in up_ring]

    def onward(value):
        return lax.ppermute(value, "mp", up_ring)

    def backward_on(value):
        return lax.ppermute(value, "mp", down_ring)

    evens = range(2, n_dp, 2)
    cuts = list(range(0, rows + 1, BLK))

    def fetch(hidden, piece):
        held = {0: hidden[cuts[piece] : cuts[piece + 1]]}
        bit = 2
        while bit < n_dp:
            for r in list(held):
                held[r ^ bit] = exchange(held[r], bit)
            bit *= 2
        return {r: held[r] for r in evens}

    def pass_on(fetched):
        return {r + 1: exchange(fetched[r], 1) for r in evens}

    far_steps = [1 << k for k in range(n_mp.bit_length() - 2, -1, -1)]
    sum_steps = [far_steps[:-2], far_steps[-2:-1], far_steps[-1:]]

    def sum_step(value, index):
        for bit in sum_steps[index]:
            value = value + exchange(value.astype(BF16), bit, "mp").astype(F32)
        return value

    (masked_grad,) = call(
        mask_kernel, "mask", [at, live_rows], [output_grad], [like(output_grad.shape, BF16)]
    )
    swapped = swap_places(masked_grad)
    near = exchange(hidden, 1)
    adapter_up, masked_grad, at = fence(adapter_up, masked_grad, at)
    *chosen, masks = call(
        functools.partial(select_kernel, n_dp, owned, rank),
        "select",
        [at, adapter_per_block],
        [adapter_up],
        [like((rank, width), BF16)] * n_dp + [like((n_dp, blocks, BLK, owned * rank), BF16)],
    )
    arrived_up = [exchange(chosen[r], r) if r else chosen[0] for r in range(n_dp)]
    turned_factor = jnp.transpose(adapter_down, (0, 2, 1)).reshape(owned * rank, units)
    factor = turned_factor.T
    swapped, near, arrived_up, factor, masks, hidden = fence(
        swapped, near, arrived_up, factor, masks, hidden
    )

    def forward(groups, span, hids, total):
        return forward_part(groups, span, hids, down_weight, factor, masks, total, q, rank)

    def forward_pairs(span, piece, total):
        for r in evens:
            hids = [fetched[p][r] for p in piece] + [passed[p][r + 1] for p in piece]
            total, pair = forward((r, 2), span, hids, total)
            for g in range(2):
                picked.setdefault(r + g, []).append(pair[g])
        return total

    offsets = [0] + [sign * step for step in range(1, half) for sign in (-1, 1)] + [half]
    ahead = behind = swapped
    ring_blocks = [swapped]
    picked = {}
    ahead, behind = onward(ahead), backward_on(behind)
    fetched = [fetch(hidden, 0)]
    up_sum, block_up = call(
        functools.partial(up_kernel, n_dp, owned),
        "up_part",
        [at, adapter_per_block],
        [masked_grad, *arrived_up],
        [like((blocks * rank, BLK), F32), like((blocks, rank, width), BF16)],
    )
    up_sum, hidden = fence(up_sum, hidden)
    up_sum = sum_step(up_sum, 0)
    total, own = forward((0, 1), (0, blocks), [hidden], None)
    picked[0] = [own[0]]
    ahead, behind, fetched[0], total, up_sum, hidden = fence(
        ahead, behind, fetched[0], total, up_sum, hidden
    )
    ring_blocks += [ahead, behind]
    ahead, behind = onward(ahead), backward_on(behind)
    fetched.append(fetch(hidden, 1))
    passed = [pass_on(fetched[0])]
    up_sum = sum_step(up_sum, 1)
    total, own = forward((1, 1), (0, blocks), [near], total)
    picked[1] = [own[0]]
    ahead, behind, fetched[1], passed, total, up_sum, hidden = fence(
        ahead, behind, fetched[1], passed, total, up_sum, hidden
    )
    ring_blocks += [ahead, behind]
    for _ in range(3, half):
        ahead, behind = onward(ahead), backward_on(behind)
        ring_blocks += [ahead, behind]
    fetched.append(fetch(hidden, 2))
    passed.append(pass_on(fetched[1]))
    total = forward_pairs((0, 2), (0, 1), total)
    total, up_sum = fence(total, up_sum)
    up_sum = sum_step(up_sum, 2)
    ahead, behind, fetched[2], passed, total, up_act = fence(
        ahead, behind, fetched[2], passed, total, up_sum.astype(BF16)
    )
    ring_blocks[-2:] = [ahead, behind]
    last = [onward(ahead[:top]), backward_on(behind[top:])]
    passed.append(pass_on(fetched[2]))
    passed, up_act = fence(passed, up_act)
    acts = [exchange(up_act, r) if r else up_act for r in range(n_dp)]
    total = forward_pairs((2, 1), (2,), total)
    last, acts, total, picked = fence(last, acts, total, picked)
    ring_blocks += last
    total = total.reshape(n_dp, q, rows, width)

    def backward(group, acts, others=(), pieces=(rows,)):
        return backward_part(
            group,
            at,
            ring_blocks,
            offsets,
            acts[group],
            masks,
            down_weight,
            turned_factor,
            n_mp,
            others,
            pieces,
        )

    def add_and_send(step, ahead, behind, *others, halves=False):
        ahead, behind = ring_add(step, at, total, ahead, behind, n_mp, halves)
        ahead, behind, *others = fence(ahead, behind, *others)
        return onward(ahead), backward_on(behind), *others

    ends = [0, 3 * rows // 8, 3 * rows // 4, rows]
    pieces = [b - a for a, b in zip(ends, ends[1:])]

    def partial_gradient(piece):
        held = {r: parts[r][piece] for r in evens}
        sent = []
        bit = n_dp // 2
        while bit > 1:
            for r in [r for r in held if r & bit]:
                value = exchange(held.pop(r), bit)
                if r == bit:
                    sent.append(value)
                else:
                    held[r ^ bit] = held[r ^ bit] + value
            bit //= 2
        return sent

    ahead, behind = opposite(at, total, n_mp)
    ahead, behind, acts = fence(ahead, behind, acts)
    ahead, behind = onward(ahead), backward_on(behind)
    held = {r: jnp.concatenate(picked[r], axis=0) for r in range(n_dp)}
    bit = 1
    while bit < n_dp:
        sent = [r for r in held if r & bit]
        arrived = exchange(jnp.concatenate([held.pop(r).astype(BF16) for r in sent]), bit)
        for index, r in enumerate(sent):
            size = blocks * rank
            piece = arrived[index * size : (index + 1) * size]
            held[r ^ bit] = held[r ^ bit].astype(F32) + piece.astype(F32)
        bit *= 2
    down_sum = held[0]
    parts = {}
    for r in evens:
        (parts[r + 1],) = backward(r + 1, acts)
    ahead, behind, parts, down_sum, acts = fence(ahead, behind, parts, down_sum, acts)
    ahead, behind, acts, parts = add_and_send(
        half - 1, ahead, behind, acts, parts, halves=True
    )
    for r in evens:
        parts[r] = backward(r, acts, [exchange(parts.pop(r + 1), 1)], pieces)
    parts, down_sum = fence(parts, down_sum)
    down_sum = sum_step(down_sum, 0)
    ahead, behind, parts, down_sum, acts = fence(ahead, behind, parts, down_sum, acts)
    arriving = [partial_gradient(0)]
    ahead, behind, acts = add_and_send(half - 2, ahead, behind, acts)
    down_sum = sum_step(down_sum, 1)
    (parts[1],) = backward(1, acts)
    ahead, behind, parts, arriving, down_sum, acts = fence(
        ahead, behind, parts, arriving, down_sum, acts
    )
    arriving.append(partial_gradient(1))
    for step in range(half - 3, 0, -1):
        ahead, behind, acts = add_and_send(step, ahead, behind, acts)
    down_sum = sum_step(down_sum, 2)
    parts[1] = exchange(parts[1], 1)
    (parts[0],) = backward(0, acts)
    ahead, behind, parts, arriving, down_sum, acts = fence(
        ahead, behind, parts, arriving, down_sum, acts
    )

    base_out = last_add(at, live_rows, total, ahead, behind, n_mp)
    branch, *terms = call(
        functools.partial(term_kernel, n_dp, owned),
        "term_up",
        [at, adapter_per_block, live_rows],
        [down_sum, masked_grad, block_up],
        [like((rows, width), F32)] + [like((rank, width), BF16)] * n_dp,
    )
    base_out, terms, parts, acts = fence(base_out, terms, parts, acts)
    base_out = swap_places(base_out)
    terms = [exchange(terms[r], r) if r else terms[0] for r in range(n_dp)]
    arriving.append(partial_gradient(2))
    hidden_gradient = blank((rows, units), BF16)
    for piece in range(2):
        hidden_gradient = combine(
            ends[piece], parts[0], parts[1], arriving[piece], hidden_gradient
        )
    groups = [hidden, near]
    for r in evens:
        groups += [piece[r] for piece in fetched] + [piece[r + 1] for piece in passed]
    down_grad = factor_grad(masks, acts, groups)
    down_grad = jnp.transpose(down_grad.reshape(owned, rank, units), (0, 2, 1))
    base_out, terms, arriving[2], hidden_gradient, down_grad, branch = fence(
        base_out, terms, arriving[2], hidden_gradient, down_grad, branch
    )
    (up_grad,) = call(
        functools.partial(up_grad_kernel, n_dp, blocks),
        "up_grad",
        [at, adapter_per_block],
        terms,
        [like((owned, rank, width), BF16)],
    )
    layer_out = (base_out.astype(F32) + branch).astype(BF16)
    hidden_gradient = combine(ends[2], parts[0], parts[1], arriving[2], hidden_gradient)
    return layer_out, hidden_gradient, down_grad, up_grad


def solution(mesh):
    return jax.shard_map(
        shards,
        mesh=mesh,
        in_specs=(
            P("dp", "mp"),
            P("mp", "dp"),
            P("dp", "mp", None),
            P("dp", None, "mp"),
            P("dp", "mp"),
            P(),
            P(),
        ),
        out_specs=(P("dp", "mp"), P("dp", "mp"), P("dp", "mp", None), P("dp", None, "mp")),
        check_vma=False,
    )
```

```python
import functools

import jax
import jax.numpy as jnp
from jax import lax
from jax.experimental import pallas as pl
from jax.experimental.pallas import tpu as pltpu
from jax.sharding import PartitionSpec as P

BLK = 128
LOW, HIGH = 2, 8
F32 = jnp.float32
BF16 = jnp.bfloat16
VMEM_LIMIT = 44 * 1024 * 1024


TURNED = (((1,), (1,)), ((), ()))
FIRSTS = (((0,), (0,)), ((), ()))


def params():
    return pltpu.CompilerParams(vmem_limit_bytes=VMEM_LIMIT)


def cost(flops):
    return pl.CostEstimate(flops=int(flops), bytes_accessed=0, transcendentals=0)


def whole(shape):
    return pl.BlockSpec(shape, lambda *_: (0,) * len(shape))


def call(kernel, name, scalars, operands, out_shapes, scratch_shapes=()):
    return pl.pallas_call(
        kernel,
        grid_spec=pltpu.PrefetchScalarGridSpec(
            num_scalar_prefetch=len(scalars),
            grid=(1,),
            in_specs=[whole(x.shape) for x in operands],
            out_specs=[whole(x.shape) for x in out_shapes],
            scratch_shapes=list(scratch_shapes),
        ),
        out_shape=list(out_shapes),
        compiler_params=params(),
        name=name,
    )(*scalars, *operands)


def mask_kernel(at_ref, live_ref, grad_ref, out_ref):
    row = lax.broadcasted_iota(jnp.int32, grad_ref.shape, 0)
    grad = grad_ref[...]
    out_ref[...] = jnp.where(row < live_ref[at_ref[0]], grad, jnp.zeros_like(grad))


def select_kernel(n_dp, owned, rank, at_ref, id_ref, up_ref, *out_refs):
    mask_ref = out_refs[-1]
    dp = at_ref[0]
    blocks = mask_ref.shape[1]
    column = lax.broadcasted_iota(jnp.int32, (BLK, owned * rank), 1)
    for r in range(n_dp):
        chosen = jnp.int32(0)
        for b in range(blocks):
            local = id_ref[(dp ^ r) * blocks + b] - dp * owned
            chosen = jnp.where((local >= 0) & (local < owned), local, chosen)
            hit = (column >= local * rank) & (column < (local + 1) * rank)
            mask_ref[r, b] = jnp.where(hit, 1.0, 0.0).astype(BF16)
        out_refs[r][...] = up_ref[chosen]


def up_kernel(n_dp, owned, at_ref, id_ref, grad_ref, *refs):
    part_ref, block_ref = refs[n_dp:]
    dp = at_ref[0]
    blocks, rank, _ = block_ref.shape
    for b in range(blocks):
        source = (id_ref[dp * blocks + b] // owned) ^ dp
        for r in range(n_dp):

            @pl.when(source == r)
            def _():
                block_ref[b] = refs[r][...]

    for b in range(blocks):
        part_ref[b * rank : (b + 1) * rank, :] = lax.dot_general(
            block_ref[b],
            grad_ref[b * BLK : (b + 1) * BLK, :],
            TURNED,
            preferred_element_type=F32,
        )


def term_kernel(
    n_dp, owned, at_ref, id_ref, live_ref, down_ref, grad_ref, block_ref, branch_ref, *out_refs
):
    dp = at_ref[0]
    blocks, rank, width = block_ref.shape
    down_act = down_ref[...].astype(BF16)
    row = lax.broadcasted_iota(jnp.int32, (BLK, width), 0)
    for r in range(n_dp):
        out_refs[r][...] = jnp.zeros(out_refs[r].shape, BF16)
    for b in range(blocks):
        rows = slice(b * BLK, (b + 1) * BLK)
        act = down_act[b * rank : (b + 1) * rank]
        branch = lax.dot_general(act, block_ref[b], FIRSTS, preferred_element_type=F32)
        branch_ref[rows, :] = jnp.where(row + b * BLK < live_ref[dp], branch, 0.0)
        term = jnp.dot(act, grad_ref[rows, :], preferred_element_type=F32).astype(BF16)
        owner = (id_ref[dp * blocks + b] // owned) ^ dp
        for r in range(n_dp):

            @pl.when(owner == r)
            def _():
                out_refs[r][...] = term


def up_grad_kernel(n_dp, blocks, at_ref, id_ref, *refs):
    out_ref = refs[n_dp]
    dp = at_ref[0]
    owned = out_ref.shape[0]
    for a in range(owned):
        total = jnp.zeros(out_ref.shape[1:], F32)
        for r in range(n_dp):
            uses = jnp.int32(0)
            for b in range(blocks):
                uses += (id_ref[(dp ^ r) * blocks + b] == dp * owned + a).astype(jnp.int32)
            total += jnp.where(uses > 0, refs[r][...].astype(F32), 0.0)
        out_ref[a] = total.astype(BF16)


def ring_slot(offset, at, n_dp, n_mp):
    dp, mp = at[0], at[1]
    place = jnp.where(mp % 2 == 0, mp // 2, n_mp - 1 - mp // 2)
    there = (place + offset + n_mp) % n_mp
    index = jnp.where(there < n_mp // 2, 2 * there, 2 * (n_mp - 1 - there) + 1)
    q = n_mp // n_dp
    return (index // q) ^ dp, index % q


def add_kernel(at_ref, a_ref, b_ref, ahead_ref, behind_ref, a_out, b_out):
    a_out[...] = (a_ref[0, 0].astype(F32) + ahead_ref[...].astype(F32)).astype(BF16)
    b_out[...] = (b_ref[0, 0].astype(F32) + behind_ref[...].astype(F32)).astype(BF16)


def half_add_kernel(at_ref, a_ref, b_ref, ahead_ref, behind_ref, a_out, b_out):
    first = pl.program_id(0) == 0

    @pl.when(first)
    def _():
        a_out[...] = (a_ref[0, 0].astype(F32) + ahead_ref[...].astype(F32)).astype(BF16)
        b_out[...] = b_ref[0, 0]

    @pl.when(jnp.logical_not(first))
    def _():
        a_out[...] = a_ref[0, 0]
        b_out[...] = (b_ref[0, 0].astype(F32) + behind_ref[...].astype(F32)).astype(BF16)


def ring_add(step, at, total, ahead, behind, n_mp, halves):
    n_dp, _, rows, width = total.shape
    top = rows // 2

    def slot(offset):
        def index(i, at_ref):
            group, part = ring_slot(offset, at_ref, n_dp, n_mp)
            return group, part, i, 0

        return pl.BlockSpec((1, 1, top, width), index)

    arrived = pl.BlockSpec((top, width), lambda i, at_ref: (0 if halves else i, 0))
    sent = pl.BlockSpec((top, width), lambda i, at_ref: (i, 0))
    return pl.pallas_call(
        half_add_kernel if halves else add_kernel,
        grid_spec=pltpu.PrefetchScalarGridSpec(
            num_scalar_prefetch=1,
            grid=(2,),
            in_specs=[slot(step), slot(-step), arrived, arrived],
            out_specs=[sent, sent],
        ),
        out_shape=[jax.ShapeDtypeStruct((rows, width), BF16)] * 2,
        compiler_params=params(),
        name="ring_add",
    )(at, total, total, ahead, behind)


def opposite_kernel(at_ref, total_ref, first_ref, second_ref):
    top = first_ref.shape[0]
    first_ref[...] = total_ref[0, 0, :top]
    second_ref[...] = total_ref[0, 0, top:]


def opposite(at, total, n_mp):
    n_dp, _, rows, width = total.shape

    def index(i, at_ref):
        group, part = ring_slot(n_mp // 2, at_ref, n_dp, n_mp)
        return group, part, 0, 0

    out = pl.BlockSpec((rows // 2, width), lambda i, at_ref: (0, 0))
    return pl.pallas_call(
        opposite_kernel,
        grid_spec=pltpu.PrefetchScalarGridSpec(
            num_scalar_prefetch=1,
            grid=(1,),
            in_specs=[pl.BlockSpec((1, 1, rows, width), index)],
            out_specs=[out, out],
        ),
        out_shape=[jax.ShapeDtypeStruct((rows // 2, width), BF16)] * 2,
        compiler_params=params(),
        name="opposite",
    )(at, total)


def last_add_kernel(n_dp, n_mp, at_ref, live_ref, own_ref, ahead_ref, behind_ref, out_ref):
    total = own_ref[0, 0].astype(F32) + ahead_ref[...].astype(F32) + behind_ref[...].astype(F32)
    row = lax.broadcasted_iota(jnp.int32, total.shape, 0) + pl.program_id(0) * total.shape[0]
    live = live_ref[at_ref[1] // (n_mp // n_dp)]
    out_ref[...] = jnp.where(row < live, total, 0.0).astype(BF16)


def last_add(at, live_rows, total, ahead, behind, n_mp):
    n_dp, _, rows, width = total.shape

    def index(i, at_ref, live_ref):
        group, part = ring_slot(0, at_ref, n_dp, n_mp)
        return group, part, i, 0

    half = pl.BlockSpec((rows // 2, width), lambda i, at_ref, live_ref: (i, 0))
    return pl.pallas_call(
        functools.partial(last_add_kernel, n_dp, n_mp),
        grid_spec=pltpu.PrefetchScalarGridSpec(
            num_scalar_prefetch=2,
            grid=(2,),
            in_specs=[pl.BlockSpec((1, 1, rows // 2, width), index), half, half],
            out_specs=half,
        ),
        out_shape=jax.ShapeDtypeStruct((rows, width), BF16),
        compiler_params=params(),
        name="last_add",
    )(at, live_rows, total, ahead, behind)


def combine_kernel(own_ref, *refs):
    total = own_ref[...].astype(F32)
    for ref in refs[:-2]:
        total += ref[...].astype(F32)
    refs[-1][...] = total.astype(BF16)


def combine(start, own, near, arrived, out):
    rows, units = own.shape
    tile = 48
    first = start // tile
    placed = pl.BlockSpec((tile, units), lambda i: (i + first, 0))
    piece = pl.BlockSpec((tile, units), lambda i: (i, 0))
    return pl.pallas_call(
        combine_kernel,
        grid=(arrived[0].shape[0] // tile,),
        in_specs=[placed, placed]
        + [piece] * len(arrived)
        + [pl.BlockSpec(memory_space=pl.ANY)],
        out_specs=placed,
        out_shape=jax.ShapeDtypeStruct((rows, units), BF16),
        input_output_aliases={2 + len(arrived): 0},
        compiler_params=params(),
        name="combine",
    )(own, near, *arrived, out)


def blank_kernel(out_ref):
    pass


def blank(shape, dtype):
    return pl.pallas_call(
        blank_kernel,
        out_specs=pl.BlockSpec(memory_space=pl.ANY),
        out_shape=jax.ShapeDtypeStruct(shape, dtype),
        name="blank",
    )()


def forward_kernel(count, *refs):
    w_ref, a_ref, m_ref = refs[count : count + 3]
    y_ref, p_ref = refs[-2:]
    hid = jnp.concatenate([ref[...] for ref in refs[:count]], axis=0)
    out = jnp.dot(hid, w_ref[...], preferred_element_type=F32).astype(BF16)
    groups, _, blocks, _, tile = y_ref.shape
    y_ref[:, 0] = out.reshape(groups, blocks, BLK, tile)

    @pl.when(pl.program_id(0) == 0)
    def _():
        ranks = a_ref.shape[1]
        rank = p_ref.shape[1] // blocks
        part = jnp.dot(hid, a_ref[...], preferred_element_type=F32)
        part = jnp.where(m_ref[...].reshape(part.shape) > 0, part, 0.0)
        picked = part[:, :rank]
        for a in range(1, ranks // rank):
            picked = picked + part[:, a * rank : (a + 1) * rank]
        picked = picked.astype(BF16)
        row = lax.broadcasted_iota(jnp.int32, (BLK, BLK), 0)
        column = lax.broadcasted_iota(jnp.int32, (BLK, BLK), 1)
        unit = jnp.where(row == column, 1.0, 0.0).astype(BF16)
        for g in range(groups):
            for b in range(blocks):
                start = (g * blocks + b) * BLK
                p_ref[g, b * rank : (b + 1) * rank, :] = lax.dot_general(
                    picked[start : start + BLK], unit, FIRSTS, preferred_element_type=F32
                ).astype(BF16)


def forward_part(groups, blocks, hids, weight, factor, masks, total, q, rank):
    units, cols = weight.shape
    n_dp, all_blocks, _, ranks = masks.shape
    width = cols // q
    tile = min(512, width)
    per = width // tile
    group, block = groups[0] // groups[1], blocks[0] // blocks[1]
    in_specs = [whole(hid.shape) for hid in hids] + [
        pl.BlockSpec((units, tile), lambda i: (0, i)),
        whole((units, ranks)),
        pl.BlockSpec((groups[1], blocks[1], BLK, ranks), lambda i: (group, block, 0, 0)),
    ]
    operands = [*hids, weight, factor, masks]
    aliases = {}
    if total is not None:
        aliases = {len(operands): 0}
        in_specs.append(pl.BlockSpec(memory_space=pl.ANY))
        operands.append(total)
    turned = (groups[1], blocks[1] * rank, BLK)
    return pl.pallas_call(
        functools.partial(forward_kernel, len(hids)),
        grid=(cols // tile,),
        in_specs=in_specs,
        out_specs=[
            pl.BlockSpec(
                (groups[1], 1, blocks[1], BLK, tile),
                lambda i: (group, i // per, block, 0, i % per),
            ),
            whole(turned),
        ],
        out_shape=[
            jax.ShapeDtypeStruct((n_dp, q, all_blocks, BLK, width), BF16),
            jax.ShapeDtypeStruct(turned, BF16),
        ],
        input_output_aliases=aliases,
        cost_estimate=cost(LOW * groups[1] * blocks[1] * BLK * units * cols),
        compiler_params=params(),
        name="forward_part",
    )(*operands)


def spread(act, mask):
    blocks, _, ranks = mask.shape
    rank = act.shape[0] // blocks
    row = lax.broadcasted_iota(jnp.int32, (rank, ranks), 0)
    column = lax.broadcasted_iota(jnp.int32, (rank, ranks), 1)
    repeat = jnp.where(column % rank == row, 1.0, 0.0).astype(BF16)
    wide = [
        lax.dot_general(
            act[b * rank : (b + 1) * rank], repeat, FIRSTS, preferred_element_type=F32
        )
        for b in range(blocks)
    ]
    wide = jnp.concatenate(wide, axis=0)
    return jnp.where(mask.reshape(wide.shape) > 0, wide, 0.0).astype(BF16)


def backward_kernel(group, n_mp, offsets, more, at_ref, *refs):
    slots = len(offsets)
    block_refs = refs[: slots + 1]
    act_ref, m_ref, w_ref, a_ref = refs[slots + 1 : slots + 5]
    z_refs = refs[slots + 5 + more : -3]
    g_ref, u_ref, sems = refs[-3:]
    q, rows, _ = g_ref.shape
    n_dp = n_mp // q
    top = rows // 2

    def transfers(act):
        for index in range(slots + 1):
            there, part = ring_slot(offsets[min(index, slots - 1)], at_ref, n_dp, n_mp)
            target = g_ref.at[part]
            if index >= slots - 1:
                target = target.at[pl.ds(top * (index - slots + 1), top)]
            copy = pltpu.make_async_copy(block_refs[index], target, sems.at[index])
            pl.when(there == group)(copy.start if act else copy.wait)

    @pl.when(pl.program_id(0) == 0)
    def _():
        transfers(True)
        u_ref[...] = spread(act_ref[...], m_ref[0])
        transfers(False)

    out = lax.dot_general(
        jnp.concatenate([g_ref[h] for h in range(q)], axis=1),
        w_ref[...],
        TURNED,
        preferred_element_type=F32,
    )
    out += jnp.dot(u_ref[...], a_ref[...], preferred_element_type=F32)
    for ref in refs[slots + 5 : slots + 5 + more]:
        out += ref[...].astype(F32)
    start = 0
    for z_ref in z_refs:
        size = z_ref.shape[0]
        z_ref[...] = out[start : start + size].astype(BF16)
        start += size


def backward_part(
    group, at, blocks, offsets, act, masks, weight, turned_factor, n_mp, others, pieces
):
    units, cols = weight.shape
    n_dp, parts, _, ranks = masks.shape
    rows = parts * BLK
    q = n_mp // n_dp
    tile = min(896, units)
    columns = lambda i, at_ref: (0, i)
    return pl.pallas_call(
        functools.partial(backward_kernel, group, n_mp, offsets, len(others)),
        grid_spec=pltpu.PrefetchScalarGridSpec(
            num_scalar_prefetch=1,
            grid=(pl.cdiv(units, tile),),
            in_specs=[pl.BlockSpec(memory_space=pl.ANY)] * len(blocks)
            + [
                whole(act.shape),
                pl.BlockSpec((1, parts, BLK, ranks), lambda i, at_ref: (group, 0, 0, 0)),
                pl.BlockSpec((tile, cols), lambda i, at_ref: (i, 0)),
                pl.BlockSpec((ranks, tile), columns),
            ]
            + [pl.BlockSpec((rows, tile), columns)] * len(others),
            out_specs=[pl.BlockSpec((size, tile), columns) for size in pieces],
            scratch_shapes=[
                pltpu.VMEM((q, rows, cols // q), BF16),
                pltpu.VMEM((rows, ranks), BF16),
                pltpu.SemaphoreType.DMA((len(blocks),)),
            ],
        ),
        out_shape=[jax.ShapeDtypeStruct((size, units), BF16) for size in pieces],
        cost_estimate=cost((HIGH if others else LOW) * rows * units * cols),
        compiler_params=params(),
        name="backward_part",
    )(at, *blocks, act, masks, weight, turned_factor, *others)


def factor_grad_kernel(n_dp, m_ref, *refs):
    acts = [spread(refs[r][...], m_ref[r]) for r in range(n_dp)]
    hid = jnp.concatenate([ref[...] for ref in refs[n_dp:-1]], axis=0)
    out = lax.dot_general(
        jnp.concatenate(acts, axis=0), hid, FIRSTS, preferred_element_type=F32
    )
    refs[-1][...] = out.astype(BF16)


def factor_grad(masks, acts, hids):
    ranks = masks.shape[3]
    units = hids[0].shape[1]
    tile = units // 2 if units % 256 == 0 else units
    return pl.pallas_call(
        functools.partial(factor_grad_kernel, len(acts)),
        grid=(units // tile,),
        in_specs=[whole(masks.shape)]
        + [whole(act.shape) for act in acts]
        + [pl.BlockSpec((hid.shape[0], tile), lambda i: (0, i)) for hid in hids],
        out_specs=pl.BlockSpec((ranks, tile), lambda i: (0, i)),
        out_shape=jax.ShapeDtypeStruct((ranks, units), BF16),
        compiler_params=params(),
        name="factor_grad",
    )(masks, *acts, *hids)


def shards(
    hidden, down_weight, adapter_down, adapter_up, output_grad, adapter_per_block, live_rows
):
    n_dp = lax.axis_size("dp")
    n_mp = lax.axis_size("mp")
    at = jnp.stack([lax.axis_index("dp"), lax.axis_index("mp")])
    q = n_mp // n_dp
    rows, units = hidden.shape
    width = output_grad.shape[1]
    owned, _, rank = adapter_down.shape
    blocks = rows // BLK
    half = n_mp // 2
    top = rows // 2
    fence = lambda *values: lax.optimization_barrier(values)
    like = jax.ShapeDtypeStruct

    def exchange(value, bit, axis="dp"):
        count = n_dp if axis == "dp" else n_mp
        return lax.ppermute(value, axis, [(i, i ^ bit) for i in range(count)])

    def swap_places(value):
        pairs = [
            (j * n_mp + m, (m // q) * n_mp + j * q + m % q)
            for j in range(n_dp)
            for m in range(n_mp)
        ]
        return lax.ppermute(value, ("dp", "mp"), pairs)

    ring = list(range(0, n_mp, 2)) + list(range(n_mp - 1, 0, -2))
    up_ring = [(ring[i], ring[(i + 1) % n_mp]) for i in range(n_mp)]
    down_ring = [(b, a) for a, b in up_ring]

    def onward(value):
        return lax.ppermute(value, "mp", up_ring)

    def backward_on(value):
        return lax.ppermute(value, "mp", down_ring)

    evens = range(2, n_dp, 2)
    cuts = list(range(0, rows + 1, BLK))

    def fetch(hidden_cut, piece):
        held = {0: hidden_cut[piece]}
        bit = 2
        while bit < n_dp:
            for r in list(held):
                held[r ^ bit] = exchange(held[r], bit)
            bit *= 2
        return {r: held[r] for r in evens}

    def pass_on(fetched):
        return {r + 1: exchange(fetched[r], 1) for r in evens}

    far_steps = [1 << k for k in range(n_mp.bit_length() - 2, -1, -1)]
    sum_steps = [far_steps[:-2], far_steps[-2:-1], far_steps[-1:]]

    def sum_step(value, index):
        for bit in sum_steps[index]:
            value = value + exchange(value.astype(BF16), bit, "mp").astype(F32)
        return value

    (masked_grad,) = call(
        mask_kernel, "mask", [at, live_rows], [output_grad], [like(output_grad.shape, BF16)]
    )
    swapped = swap_places(masked_grad)
    near = exchange(hidden, 1)
    adapter_up, masked_grad, at = fence(adapter_up, masked_grad, at)
    *chosen, masks = call(
        functools.partial(select_kernel, n_dp, owned, rank),
        "select",
        [at, adapter_per_block],
        [adapter_up],
        [like((rank, width), BF16)] * n_dp + [like((n_dp, blocks, BLK, owned * rank), BF16)],
    )
    arrived_up = [exchange(chosen[r], r) if r else chosen[0] for r in range(n_dp)]
    turned_factor = jnp.transpose(adapter_down, (0, 2, 1)).reshape(owned * rank, units)
    factor = turned_factor.T
    hidden_cut = [hidden[a:b] for a, b in zip(cuts, cuts[1:])]
    swapped, near, arrived_up, factor, masks, hidden, hidden_cut = fence(
        swapped, near, arrived_up, factor, masks, hidden, hidden_cut
    )

    def forward(groups, span, hids, total):
        return forward_part(groups, span, hids, down_weight, factor, masks, total, q, rank)

    def forward_pairs(span, piece, total):
        for r in evens:
            hids = [fetched[p][r] for p in piece] + [passed[p][r + 1] for p in piece]
            total, pair = forward((r, 2), span, hids, total)
            for g in range(2):
                picked.setdefault(r + g, []).append(pair[g])
        return total

    offsets = [0] + [sign * step for step in range(1, half) for sign in (-1, 1)] + [half]
    ahead = behind = swapped
    ring_blocks = [swapped]
    picked = {}
    ahead, behind = onward(ahead), backward_on(behind)
    fetched = [fetch(hidden_cut, 0)]
    up_sum, block_up = call(
        functools.partial(up_kernel, n_dp, owned),
        "up_part",
        [at, adapter_per_block],
        [masked_grad, *arrived_up],
        [like((blocks * rank, BLK), F32), like((blocks, rank, width), BF16)],
    )
    up_sum, hidden = fence(up_sum, hidden)
    up_sum = sum_step(up_sum, 0)
    total, own = forward((0, 1), (0, blocks), [hidden], None)
    picked[0] = [own[0]]
    ahead, behind, fetched[0], total, up_sum, hidden_cut = fence(
        ahead, behind, fetched[0], total, up_sum, hidden_cut
    )
    ring_blocks += [ahead, behind]
    ahead, behind = onward(ahead), backward_on(behind)
    fetched.append(fetch(hidden_cut, 1))
    passed = [pass_on(fetched[0])]
    up_sum = sum_step(up_sum, 1)
    total, own = forward((1, 1), (0, blocks), [near], total)
    picked[1] = [own[0]]
    ahead, behind, fetched[1], passed, total, up_sum, hidden_cut = fence(
        ahead, behind, fetched[1], passed, total, up_sum, hidden_cut
    )
    ring_blocks += [ahead, behind]
    for _ in range(3, half):
        ahead, behind = onward(ahead), backward_on(behind)
        ring_blocks += [ahead, behind]
    fetched.append(fetch(hidden_cut, 2))
    passed.append(pass_on(fetched[1]))
    total = forward_pairs((0, 2), (0, 1), total)
    total, up_sum = fence(total, up_sum)
    up_sum = sum_step(up_sum, 2)
    ahead, behind, fetched[2], passed, total, up_act = fence(
        ahead, behind, fetched[2], passed, total, up_sum.astype(BF16)
    )
    ring_blocks[-2:] = [ahead, behind]
    last = [onward(ahead[:top]), backward_on(behind[top:])]
    passed.append(pass_on(fetched[2]))
    passed, up_act = fence(passed, up_act)
    acts = [exchange(up_act, r) if r else up_act for r in range(n_dp)]
    total = forward_pairs((2, 1), (2,), total)
    last, acts, total, picked = fence(last, acts, total, picked)
    ring_blocks += last
    total = total.reshape(n_dp, q, rows, width)

    def backward(group, acts, others=(), pieces=(rows,)):
        return backward_part(
            group,
            at,
            ring_blocks,
            offsets,
            acts[group],
            masks,
            down_weight,
            turned_factor,
            n_mp,
            others,
            pieces,
        )

    def add_and_send(step, ahead, behind, *others, halves=False):
        ahead, behind = ring_add(step, at, total, ahead, behind, n_mp, halves)
        ahead, behind, *others = fence(ahead, behind, *others)
        return onward(ahead), backward_on(behind), *others

    ends = [0, 3 * rows // 8, 3 * rows // 4, rows]
    pieces = [b - a for a, b in zip(ends, ends[1:])]

    def partial_gradient(piece, parts):
        held = {r: parts[r][piece] for r in evens}
        sent = []
        bit = n_dp // 2
        while bit > 1:
            for r in [r for r in held if r & bit]:
                value = exchange(held.pop(r), bit)
                if r == bit:
                    sent.append(value)
                else:
                    held[r ^ bit] = held[r ^ bit] + value
            bit //= 2
        return sent

    ahead, behind = opposite(at, total, n_mp)
    ahead, behind, acts = fence(ahead, behind, acts)
    ahead, behind = onward(ahead), backward_on(behind)
    held = {r: jnp.concatenate(picked[r], axis=0) for r in range(n_dp)}
    bit = 1
    while bit < n_dp:
        sent = [r for r in held if r & bit]
        arrived = exchange(jnp.concatenate([held.pop(r).astype(BF16) for r in sent]), bit)
        for index, r in enumerate(sent):
            size = blocks * rank
            piece = arrived[index * size : (index + 1) * size]
            held[r ^ bit] = held[r ^ bit].astype(F32) + piece.astype(F32)
        bit *= 2
    down_sum = held[0]
    parts = {}
    for r in evens:
        (parts[r + 1],) = backward(r + 1, acts)
    ahead, behind, parts, down_sum, acts = fence(ahead, behind, parts, down_sum, acts)
    ahead, behind, acts, parts = add_and_send(
        half - 1, ahead, behind, acts, parts, halves=True
    )
    for r in evens:
        parts[r] = backward(r, acts, [exchange(parts.pop(r + 1), 1)], pieces)
    parts, down_sum = fence(parts, down_sum)
    down_sum = sum_step(down_sum, 0)
    ahead, behind, parts, down_sum, acts = fence(ahead, behind, parts, down_sum, acts)
    arriving = [partial_gradient(0, parts)]
    ahead, behind, acts = add_and_send(half - 2, ahead, behind, acts)
    down_sum = sum_step(down_sum, 1)
    (parts[1],) = backward(1, acts)
    ahead, behind, parts, arriving, down_sum, acts = fence(
        ahead, behind, parts, arriving, down_sum, acts
    )
    arriving.append(partial_gradient(1, parts))
    for step in range(half - 3, 0, -1):
        ahead, behind, acts = add_and_send(step, ahead, behind, acts)
    down_sum = sum_step(down_sum, 2)
    parts[1] = exchange(parts[1], 1)
    (parts[0],) = backward(0, acts)
    ahead, behind, parts, arriving, down_sum, acts = fence(
        ahead, behind, parts, arriving, down_sum, acts
    )

    base_out = last_add(at, live_rows, total, ahead, behind, n_mp)
    base_out, down_sum, parts, acts = fence(base_out, down_sum, parts, acts)
    base_out = swap_places(base_out)
    branch, *terms = call(
        functools.partial(term_kernel, n_dp, owned),
        "term_up",
        [at, adapter_per_block, live_rows],
        [down_sum, masked_grad, block_up],
        [like((rows, width), F32)] + [like((rank, width), BF16)] * n_dp,
    )
    terms = [exchange(terms[r], r) if r else terms[0] for r in range(n_dp)]
    arriving.append(partial_gradient(2, parts))
    hidden_gradient = blank((rows, units), BF16)
    for piece in range(2):
        hidden_gradient = combine(
            ends[piece], parts[0], parts[1], arriving[piece], hidden_gradient
        )
    groups = [hidden, near]
    for r in evens:
        groups += [piece[r] for piece in fetched] + [piece[r + 1] for piece in passed]
    down_grad = factor_grad(masks, acts, groups)
    down_grad = jnp.transpose(down_grad.reshape(owned, rank, units), (0, 2, 1))
    terms, hidden_gradient, down_grad, branch = fence(terms, hidden_gradient, down_grad, branch)
    (up_grad,) = call(
        functools.partial(up_grad_kernel, n_dp, blocks),
        "up_grad",
        [at, adapter_per_block],
        terms,
        [like((owned, rank, width), BF16)],
    )
    base_out, arriving[2], up_grad = fence(base_out, arriving[2], up_grad)
    hidden_gradient = combine(ends[2], parts[0], parts[1], arriving[2], hidden_gradient)
    layer_out = (base_out.astype(F32) + branch).astype(BF16)
    return layer_out, hidden_gradient, down_grad, up_grad


def solution(mesh):
    return jax.shard_map(
        shards,
        mesh=mesh,
        in_specs=(
            P("dp", "mp"),
            P("mp", "dp"),
            P("dp", "mp", None),
            P("dp", None, "mp"),
            P("dp", "mp"),
            P(),
            P(),
        ),
        out_specs=(P("dp", "mp"), P("dp", "mp"), P("dp", "mp", None), P("dp", None, "mp")),
        check_vma=False,
    )
```

```python
import functools

import jax
import jax.numpy as jnp
from jax import lax
from jax.experimental import pallas as pl
from jax.experimental.pallas import tpu as pltpu
from jax.sharding import PartitionSpec as P

BLK = 128
LOW, HIGH = 2, 8
F32 = jnp.float32
BF16 = jnp.bfloat16
VMEM_LIMIT = 44 * 1024 * 1024


TURNED = (((1,), (1,)), ((), ()))
FIRSTS = (((0,), (0,)), ((), ()))


def params():
    return pltpu.CompilerParams(vmem_limit_bytes=VMEM_LIMIT)


def cost(flops):
    return pl.CostEstimate(flops=int(flops), bytes_accessed=0, transcendentals=0)


def whole(shape):
    return pl.BlockSpec(shape, lambda *_: (0,) * len(shape))


def call(kernel, name, scalars, operands, out_shapes, scratch_shapes=()):
    return pl.pallas_call(
        kernel,
        grid_spec=pltpu.PrefetchScalarGridSpec(
            num_scalar_prefetch=len(scalars),
            grid=(1,),
            in_specs=[whole(x.shape) for x in operands],
            out_specs=[whole(x.shape) for x in out_shapes],
            scratch_shapes=list(scratch_shapes),
        ),
        out_shape=list(out_shapes),
        compiler_params=params(),
        name=name,
    )(*scalars, *operands)


def mask_kernel(at_ref, live_ref, grad_ref, out_ref):
    row = lax.broadcasted_iota(jnp.int32, grad_ref.shape, 0)
    grad = grad_ref[...]
    out_ref[...] = jnp.where(row < live_ref[at_ref[0]], grad, jnp.zeros_like(grad))


def select_kernel(n_dp, owned, rank, at_ref, id_ref, up_ref, *out_refs):
    mask_ref = out_refs[-1]
    dp = at_ref[0]
    blocks = mask_ref.shape[1]
    column = lax.broadcasted_iota(jnp.int32, (BLK, owned * rank), 1)
    for r in range(n_dp):
        chosen = jnp.int32(0)
        for b in range(blocks):
            local = id_ref[(dp ^ r) * blocks + b] - dp * owned
            chosen = jnp.where((local >= 0) & (local < owned), local, chosen)
            hit = (column >= local * rank) & (column < (local + 1) * rank)
            mask_ref[r, b] = jnp.where(hit, 1.0, 0.0).astype(BF16)
        out_refs[r][...] = up_ref[chosen]


def up_kernel(n_dp, owned, at_ref, id_ref, grad_ref, *refs):
    part_ref, block_ref = refs[n_dp:]
    dp = at_ref[0]
    blocks, rank, _ = block_ref.shape
    for b in range(blocks):
        source = (id_ref[dp * blocks + b] // owned) ^ dp
        for r in range(n_dp):

            @pl.when(source == r)
            def _():
                block_ref[b] = refs[r][...]

    for b in range(blocks):
        part_ref[b * rank : (b + 1) * rank, :] = lax.dot_general(
            block_ref[b],
            grad_ref[b * BLK : (b + 1) * BLK, :],
            TURNED,
            preferred_element_type=F32,
        )


def term_kernel(
    n_dp, owned, at_ref, id_ref, live_ref, down_ref, grad_ref, block_ref, branch_ref, *out_refs
):
    dp = at_ref[0]
    blocks, rank, width = block_ref.shape
    down_act = down_ref[...].astype(BF16)
    row = lax.broadcasted_iota(jnp.int32, (BLK, width), 0)
    for r in range(n_dp):
        out_refs[r][...] = jnp.zeros(out_refs[r].shape, BF16)
    for b in range(blocks):
        rows = slice(b * BLK, (b + 1) * BLK)
        act = down_act[b * rank : (b + 1) * rank]
        branch = lax.dot_general(act, block_ref[b], FIRSTS, preferred_element_type=F32)
        branch_ref[rows, :] = jnp.where(row + b * BLK < live_ref[dp], branch, 0.0).astype(BF16)
        term = jnp.dot(act, grad_ref[rows, :], preferred_element_type=F32).astype(BF16)
        owner = (id_ref[dp * blocks + b] // owned) ^ dp
        for r in range(n_dp):

            @pl.when(owner == r)
            def _():
                out_refs[r][...] = term


def up_grad_kernel(n_dp, blocks, at_ref, id_ref, *refs):
    out_ref = refs[n_dp]
    dp = at_ref[0]
    owned = out_ref.shape[0]
    for a in range(owned):
        total = jnp.zeros(out_ref.shape[1:], F32)
        for r in range(n_dp):
            uses = jnp.int32(0)
            for b in range(blocks):
                uses += (id_ref[(dp ^ r) * blocks + b] == dp * owned + a).astype(jnp.int32)
            total += jnp.where(uses > 0, refs[r][...].astype(F32), 0.0)
        out_ref[a] = total.astype(BF16)


def ring_slot(offset, at, n_dp, n_mp):
    dp, mp = at[0], at[1]
    place = jnp.where(mp % 2 == 0, mp // 2, n_mp - 1 - mp // 2)
    there = (place + offset + n_mp) % n_mp
    index = jnp.where(there < n_mp // 2, 2 * there, 2 * (n_mp - 1 - there) + 1)
    q = n_mp // n_dp
    return (index // q) ^ dp, index % q


def add_kernel(at_ref, a_ref, b_ref, ahead_ref, behind_ref, a_out, b_out):
    a_out[...] = (a_ref[0, 0].astype(F32) + ahead_ref[...].astype(F32)).astype(BF16)
    b_out[...] = (b_ref[0, 0].astype(F32) + behind_ref[...].astype(F32)).astype(BF16)


def half_add_kernel(at_ref, a_ref, b_ref, ahead_ref, behind_ref, a_out, b_out):
    first = pl.program_id(0) == 0

    @pl.when(first)
    def _():
        a_out[...] = (a_ref[0, 0].astype(F32) + ahead_ref[...].astype(F32)).astype(BF16)
        b_out[...] = b_ref[0, 0]

    @pl.when(jnp.logical_not(first))
    def _():
        a_out[...] = a_ref[0, 0]
        b_out[...] = (b_ref[0, 0].astype(F32) + behind_ref[...].astype(F32)).astype(BF16)


def ring_add(step, at, total, ahead, behind, n_mp, halves):
    n_dp, _, rows, width = total.shape
    top = rows // 2

    def slot(offset):
        def index(i, at_ref):
            group, part = ring_slot(offset, at_ref, n_dp, n_mp)
            return group, part, i, 0

        return pl.BlockSpec((1, 1, top, width), index)

    arrived = pl.BlockSpec((top, width), lambda i, at_ref: (0 if halves else i, 0))
    sent = pl.BlockSpec((top, width), lambda i, at_ref: (i, 0))
    return pl.pallas_call(
        half_add_kernel if halves else add_kernel,
        grid_spec=pltpu.PrefetchScalarGridSpec(
            num_scalar_prefetch=1,
            grid=(2,),
            in_specs=[slot(step), slot(-step), arrived, arrived],
            out_specs=[sent, sent],
        ),
        out_shape=[jax.ShapeDtypeStruct((rows, width), BF16)] * 2,
        compiler_params=params(),
        name="ring_add",
    )(at, total, total, ahead, behind)


def opposite_kernel(at_ref, total_ref, first_ref, second_ref):
    top = first_ref.shape[0]
    first_ref[...] = total_ref[0, 0, :top]
    second_ref[...] = total_ref[0, 0, top:]


def opposite(at, total, n_mp):
    n_dp, _, rows, width = total.shape

    def index(i, at_ref):
        group, part = ring_slot(n_mp // 2, at_ref, n_dp, n_mp)
        return group, part, 0, 0

    out = pl.BlockSpec((rows // 2, width), lambda i, at_ref: (0, 0))
    return pl.pallas_call(
        opposite_kernel,
        grid_spec=pltpu.PrefetchScalarGridSpec(
            num_scalar_prefetch=1,
            grid=(1,),
            in_specs=[pl.BlockSpec((1, 1, rows, width), index)],
            out_specs=[out, out],
        ),
        out_shape=[jax.ShapeDtypeStruct((rows // 2, width), BF16)] * 2,
        compiler_params=params(),
        name="opposite",
    )(at, total)


def last_add_kernel(n_dp, n_mp, at_ref, live_ref, own_ref, ahead_ref, behind_ref, out_ref):
    total = own_ref[0, 0].astype(F32) + ahead_ref[...].astype(F32) + behind_ref[...].astype(F32)
    row = lax.broadcasted_iota(jnp.int32, total.shape, 0) + pl.program_id(0) * total.shape[0]
    live = live_ref[at_ref[1] // (n_mp // n_dp)]
    out_ref[...] = jnp.where(row < live, total, 0.0).astype(BF16)


def last_add(at, live_rows, total, ahead, behind, n_mp):
    n_dp, _, rows, width = total.shape

    def index(i, at_ref, live_ref):
        group, part = ring_slot(0, at_ref, n_dp, n_mp)
        return group, part, i, 0

    half = pl.BlockSpec((rows // 2, width), lambda i, at_ref, live_ref: (i, 0))
    return pl.pallas_call(
        functools.partial(last_add_kernel, n_dp, n_mp),
        grid_spec=pltpu.PrefetchScalarGridSpec(
            num_scalar_prefetch=2,
            grid=(2,),
            in_specs=[pl.BlockSpec((1, 1, rows // 2, width), index), half, half],
            out_specs=half,
        ),
        out_shape=jax.ShapeDtypeStruct((rows, width), BF16),
        compiler_params=params(),
        name="last_add",
    )(at, live_rows, total, ahead, behind)


def combine_kernel(own_ref, *refs):
    total = own_ref[...].astype(F32)
    for ref in refs[:-2]:
        total += ref[...].astype(F32)
    refs[-1][...] = total.astype(BF16)


def combine(start, own, near, arrived, out):
    rows, units = own.shape
    tile = 32
    first = start // tile
    placed = pl.BlockSpec((tile, units), lambda i: (i + first, 0))
    piece = pl.BlockSpec((tile, units), lambda i: (i, 0))
    return pl.pallas_call(
        combine_kernel,
        grid=(arrived[0].shape[0] // tile,),
        in_specs=[placed, placed]
        + [piece] * len(arrived)
        + [pl.BlockSpec(memory_space=pl.ANY)],
        out_specs=placed,
        out_shape=jax.ShapeDtypeStruct((rows, units), BF16),
        input_output_aliases={2 + len(arrived): 0},
        compiler_params=params(),
        name="combine",
    )(own, near, *arrived, out)


def blank_kernel(out_ref):
    pass


def blank(shape, dtype):
    return pl.pallas_call(
        blank_kernel,
        out_specs=pl.BlockSpec(memory_space=pl.ANY),
        out_shape=jax.ShapeDtypeStruct(shape, dtype),
        name="blank",
    )()


def forward_kernel(count, *refs):
    w_ref, a_ref, m_ref = refs[count : count + 3]
    y_ref, p_ref = refs[-2:]
    hid = jnp.concatenate([ref[...] for ref in refs[:count]], axis=0)
    out = jnp.dot(hid, w_ref[...], preferred_element_type=F32).astype(BF16)
    groups, _, blocks, _, tile = y_ref.shape
    y_ref[:, 0] = out.reshape(groups, blocks, BLK, tile)

    @pl.when(pl.program_id(0) == 0)
    def _():
        ranks = a_ref.shape[1]
        rank = p_ref.shape[1] // blocks
        part = jnp.dot(hid, a_ref[...], preferred_element_type=F32)
        part = jnp.where(m_ref[...].reshape(part.shape) > 0, part, 0.0)
        picked = part[:, :rank]
        for a in range(1, ranks // rank):
            picked = picked + part[:, a * rank : (a + 1) * rank]
        picked = picked.astype(BF16)
        row = lax.broadcasted_iota(jnp.int32, (BLK, BLK), 0)
        column = lax.broadcasted_iota(jnp.int32, (BLK, BLK), 1)
        unit = jnp.where(row == column, 1.0, 0.0).astype(BF16)
        for g in range(groups):
            for b in range(blocks):
                start = (g * blocks + b) * BLK
                p_ref[g, b * rank : (b + 1) * rank, :] = lax.dot_general(
                    picked[start : start + BLK], unit, FIRSTS, preferred_element_type=F32
                ).astype(BF16)


def forward_part(groups, blocks, hids, weight, factor, masks, total, q, rank):
    units, cols = weight.shape
    n_dp, all_blocks, _, ranks = masks.shape
    width = cols // q
    tile = min(512, width)
    per = width // tile
    group, block = groups[0] // groups[1], blocks[0] // blocks[1]
    in_specs = [whole(hid.shape) for hid in hids] + [
        pl.BlockSpec((units, tile), lambda i: (0, i)),
        whole((units, ranks)),
        pl.BlockSpec((groups[1], blocks[1], BLK, ranks), lambda i: (group, block, 0, 0)),
    ]
    operands = [*hids, weight, factor, masks]
    aliases = {}
    if total is not None:
        aliases = {len(operands): 0}
        in_specs.append(pl.BlockSpec(memory_space=pl.ANY))
        operands.append(total)
    turned = (groups[1], blocks[1] * rank, BLK)
    return pl.pallas_call(
        functools.partial(forward_kernel, len(hids)),
        grid=(cols // tile,),
        in_specs=in_specs,
        out_specs=[
            pl.BlockSpec(
                (groups[1], 1, blocks[1], BLK, tile),
                lambda i: (group, i // per, block, 0, i % per),
            ),
            whole(turned),
        ],
        out_shape=[
            jax.ShapeDtypeStruct((n_dp, q, all_blocks, BLK, width), BF16),
            jax.ShapeDtypeStruct(turned, BF16),
        ],
        input_output_aliases=aliases,
        cost_estimate=cost(LOW * groups[1] * blocks[1] * BLK * units * cols),
        compiler_params=params(),
        name="forward_part",
    )(*operands)


def spread(act, mask):
    blocks, _, ranks = mask.shape
    rank = act.shape[0] // blocks
    row = lax.broadcasted_iota(jnp.int32, (rank, ranks), 0)
    column = lax.broadcasted_iota(jnp.int32, (rank, ranks), 1)
    repeat = jnp.where(column % rank == row, 1.0, 0.0).astype(BF16)
    wide = [
        lax.dot_general(
            act[b * rank : (b + 1) * rank], repeat, FIRSTS, preferred_element_type=F32
        )
        for b in range(blocks)
    ]
    wide = jnp.concatenate(wide, axis=0)
    return jnp.where(mask.reshape(wide.shape) > 0, wide, 0.0).astype(BF16)


def backward_kernel(group, n_mp, offsets, more, at_ref, *refs):
    slots = len(offsets)
    block_refs = refs[: slots + 1]
    act_ref, m_ref, w_ref, a_ref = refs[slots + 1 : slots + 5]
    z_refs = refs[slots + 5 + more : -3]
    g_ref, u_ref, sems = refs[-3:]
    q, rows, _ = g_ref.shape
    n_dp = n_mp // q
    top = rows // 2

    def transfers(act):
        for index in range(slots + 1):
            there, part = ring_slot(offsets[min(index, slots - 1)], at_ref, n_dp, n_mp)
            target = g_ref.at[part]
            if index >= slots - 1:
                target = target.at[pl.ds(top * (index - slots + 1), top)]
            copy = pltpu.make_async_copy(block_refs[index], target, sems.at[index])
            pl.when(there == group)(copy.start if act else copy.wait)

    @pl.when(pl.program_id(0) == 0)
    def _():
        transfers(True)
        u_ref[...] = spread(act_ref[...], m_ref[0])
        transfers(False)

    out = lax.dot_general(
        jnp.concatenate([g_ref[h] for h in range(q)], axis=1),
        w_ref[...],
        TURNED,
        preferred_element_type=F32,
    )
    out += jnp.dot(u_ref[...], a_ref[...], preferred_element_type=F32)
    for ref in refs[slots + 5 : slots + 5 + more]:
        out += ref[...].astype(F32)
    start = 0
    for z_ref in z_refs:
        size = z_ref.shape[0]
        z_ref[...] = out[start : start + size].astype(BF16)
        start += size


def backward_part(
    group, at, blocks, offsets, act, masks, weight, turned_factor, n_mp, others, pieces
):
    units, cols = weight.shape
    n_dp, parts, _, ranks = masks.shape
    rows = parts * BLK
    q = n_mp // n_dp
    tile = min(896, units)
    columns = lambda i, at_ref: (0, i)
    return pl.pallas_call(
        functools.partial(backward_kernel, group, n_mp, offsets, len(others)),
        grid_spec=pltpu.PrefetchScalarGridSpec(
            num_scalar_prefetch=1,
            grid=(pl.cdiv(units, tile),),
            in_specs=[pl.BlockSpec(memory_space=pl.ANY)] * len(blocks)
            + [
                whole(act.shape),
                pl.BlockSpec((1, parts, BLK, ranks), lambda i, at_ref: (group, 0, 0, 0)),
                pl.BlockSpec((tile, cols), lambda i, at_ref: (i, 0)),
                pl.BlockSpec((ranks, tile), columns),
            ]
            + [pl.BlockSpec((rows, tile), columns)] * len(others),
            out_specs=[pl.BlockSpec((size, tile), columns) for size in pieces],
            scratch_shapes=[
                pltpu.VMEM((q, rows, cols // q), BF16),
                pltpu.VMEM((rows, ranks), BF16),
                pltpu.SemaphoreType.DMA((len(blocks),)),
            ],
        ),
        out_shape=[jax.ShapeDtypeStruct((size, units), BF16) for size in pieces],
        cost_estimate=cost((HIGH if others else LOW) * rows * units * cols),
        compiler_params=params(),
        name="backward_part",
    )(at, *blocks, act, masks, weight, turned_factor, *others)


def factor_grad_kernel(n_dp, m_ref, *refs):
    acts = [spread(refs[r][...], m_ref[r]) for r in range(n_dp)]
    hid = jnp.concatenate([ref[...] for ref in refs[n_dp:-1]], axis=0)
    out = lax.dot_general(
        jnp.concatenate(acts, axis=0), hid, FIRSTS, preferred_element_type=F32
    )
    refs[-1][...] = out.astype(BF16)


def factor_grad(masks, acts, hids):
    ranks = masks.shape[3]
    units = hids[0].shape[1]
    tile = units // 2 if units % 256 == 0 else units
    return pl.pallas_call(
        functools.partial(factor_grad_kernel, len(acts)),
        grid=(units // tile,),
        in_specs=[whole(masks.shape)]
        + [whole(act.shape) for act in acts]
        + [pl.BlockSpec((hid.shape[0], tile), lambda i: (0, i)) for hid in hids],
        out_specs=pl.BlockSpec((ranks, tile), lambda i: (0, i)),
        out_shape=jax.ShapeDtypeStruct((ranks, units), BF16),
        compiler_params=params(),
        name="factor_grad",
    )(masks, *acts, *hids)


def shards(
    hidden, down_weight, adapter_down, adapter_up, output_grad, adapter_per_block, live_rows
):
    n_dp = lax.axis_size("dp")
    n_mp = lax.axis_size("mp")
    at = jnp.stack([lax.axis_index("dp"), lax.axis_index("mp")])
    q = n_mp // n_dp
    rows, units = hidden.shape
    width = output_grad.shape[1]
    owned, _, rank = adapter_down.shape
    blocks = rows // BLK
    half = n_mp // 2
    top = rows // 2
    fence = lambda *values: lax.optimization_barrier(values)
    like = jax.ShapeDtypeStruct

    def exchange(value, bit, axis="dp"):
        count = n_dp if axis == "dp" else n_mp
        return lax.ppermute(value, axis, [(i, i ^ bit) for i in range(count)])

    def swap_places(value):
        pairs = [
            (j * n_mp + m, (m // q) * n_mp + j * q + m % q)
            for j in range(n_dp)
            for m in range(n_mp)
        ]
        return lax.ppermute(value, ("dp", "mp"), pairs)

    ring = list(range(0, n_mp, 2)) + list(range(n_mp - 1, 0, -2))
    up_ring = [(ring[i], ring[(i + 1) % n_mp]) for i in range(n_mp)]
    down_ring = [(b, a) for a, b in up_ring]

    def onward(value):
        return lax.ppermute(value, "mp", up_ring)

    def backward_on(value):
        return lax.ppermute(value, "mp", down_ring)

    evens = range(2, n_dp, 2)
    cuts = list(range(0, rows + 1, BLK))

    def fetch(hidden_cut, piece):
        held = {0: hidden_cut[piece]}
        bit = 2
        while bit < n_dp:
            for r in list(held):
                held[r ^ bit] = exchange(held[r], bit)
            bit *= 2
        return {r: held[r] for r in evens}

    def pass_on(fetched):
        return {r + 1: exchange(fetched[r], 1) for r in evens}

    far_steps = [1 << k for k in range(n_mp.bit_length() - 2, -1, -1)]
    sum_steps = [far_steps[:-2], far_steps[-2:-1], far_steps[-1:]]

    def sum_step(value, index):
        for bit in sum_steps[index]:
            value = value + exchange(value.astype(BF16), bit, "mp").astype(F32)
        return value

    (masked_grad,) = call(
        mask_kernel, "mask", [at, live_rows], [output_grad], [like(output_grad.shape, BF16)]
    )
    swapped = swap_places(masked_grad)
    near = exchange(hidden, 1)
    adapter_up, masked_grad, at = fence(adapter_up, masked_grad, at)
    *chosen, masks = call(
        functools.partial(select_kernel, n_dp, owned, rank),
        "select",
        [at, adapter_per_block],
        [adapter_up],
        [like((rank, width), BF16)] * n_dp + [like((n_dp, blocks, BLK, owned * rank), BF16)],
    )
    arrived_up = [exchange(chosen[r], r) if r else chosen[0] for r in range(n_dp)]
    turned_factor = jnp.transpose(adapter_down, (0, 2, 1)).reshape(owned * rank, units)
    factor = turned_factor.T
    hidden_cut = [hidden[a:b] for a, b in zip(cuts, cuts[1:])]
    def forward(groups, span, hids, total):
        return forward_part(groups, span, hids, down_weight, factor, masks, total, q, rank)

    total, own = forward((0, 1), (0, blocks), [hidden], None)
    picked = {0: [own[0]]}
    swapped, near, arrived_up, hidden, hidden_cut, total, picked = fence(
        swapped, near, arrived_up, hidden, hidden_cut, total, picked
    )

    def forward_pairs(span, piece, total):
        for r in evens:
            hids = [fetched[p][r] for p in piece] + [passed[p][r + 1] for p in piece]
            total, pair = forward((r, 2), span, hids, total)
            for g in range(2):
                picked.setdefault(r + g, []).append(pair[g])
        return total

    offsets = [0] + [sign * step for step in range(1, half) for sign in (-1, 1)] + [half]
    ahead = behind = swapped
    ring_blocks = [swapped]
    ahead, behind = onward(ahead), backward_on(behind)
    fetched = [fetch(hidden_cut, 0)]
    up_sum, block_up = call(
        functools.partial(up_kernel, n_dp, owned),
        "up_part",
        [at, adapter_per_block],
        [masked_grad, *arrived_up],
        [like((blocks * rank, BLK), F32), like((blocks, rank, width), BF16)],
    )
    up_sum = sum_step(up_sum, 0)
    ahead, behind, fetched[0], total, near, up_sum, hidden_cut = fence(
        ahead, behind, fetched[0], total, near, up_sum, hidden_cut
    )
    ring_blocks += [ahead, behind]
    ahead, behind = onward(ahead), backward_on(behind)
    fetched.append(fetch(hidden_cut, 1))
    passed = [pass_on(fetched[0])]
    up_sum = sum_step(up_sum, 1)
    total, own = forward((1, 1), (0, blocks), [near], total)
    picked[1] = [own[0]]
    ahead, behind, fetched[1], passed, total, up_sum, hidden_cut = fence(
        ahead, behind, fetched[1], passed, total, up_sum, hidden_cut
    )
    ring_blocks += [ahead, behind]
    for _ in range(3, half):
        ahead, behind = onward(ahead), backward_on(behind)
        ring_blocks += [ahead, behind]
    fetched.append(fetch(hidden_cut, 2))
    passed.append(pass_on(fetched[1]))
    total = forward_pairs((0, 2), (0, 1), total)
    total, up_sum = fence(total, up_sum)
    up_sum = sum_step(up_sum, 2)
    ahead, behind, fetched[2], passed, total, up_act = fence(
        ahead, behind, fetched[2], passed, total, up_sum.astype(BF16)
    )
    ring_blocks[-2:] = [ahead, behind]
    last = [onward(ahead[:top]), backward_on(behind[top:])]
    passed.append(pass_on(fetched[2]))
    passed, up_act = fence(passed, up_act)
    acts = [exchange(up_act, r) if r else up_act for r in range(n_dp)]
    total = forward_pairs((2, 1), (2,), total)
    last, acts, total, picked = fence(last, acts, total, picked)
    ring_blocks += last
    total = total.reshape(n_dp, q, rows, width)

    def backward(group, acts, others=(), pieces=(rows,)):
        return backward_part(
            group,
            at,
            ring_blocks,
            offsets,
            acts[group],
            masks,
            down_weight,
            turned_factor,
            n_mp,
            others,
            pieces,
        )

    def add_and_send(step, ahead, behind, *others, halves=False):
        ahead, behind = ring_add(step, at, total, ahead, behind, n_mp, halves)
        ahead, behind, *others = fence(ahead, behind, *others)
        return onward(ahead), backward_on(behind), *others

    ends = [0, 5 * rows // 12, 5 * rows // 6, rows]
    pieces = [b - a for a, b in zip(ends, ends[1:])]

    def partial_gradient(piece, parts):
        held = {r: parts[r][piece] for r in evens}
        sent = []
        bit = n_dp // 2
        while bit > 1:
            for r in [r for r in held if r & bit]:
                value = exchange(held.pop(r), bit)
                if r == bit:
                    sent.append(value)
                else:
                    held[r ^ bit] = held[r ^ bit] + value
            bit //= 2
        return sent

    ahead, behind = opposite(at, total, n_mp)
    ahead, behind, acts = fence(ahead, behind, acts)
    ahead, behind = onward(ahead), backward_on(behind)
    held = {r: jnp.concatenate(picked[r], axis=0) for r in range(n_dp)}
    bit = 1
    while bit < n_dp:
        sent = [r for r in held if r & bit]
        arrived = exchange(jnp.concatenate([held.pop(r).astype(BF16) for r in sent]), bit)
        for index, r in enumerate(sent):
            size = blocks * rank
            piece = arrived[index * size : (index + 1) * size]
            held[r ^ bit] = held[r ^ bit].astype(F32) + piece.astype(F32)
        bit *= 2
    down_sum = held[0]
    parts = {}
    for r in evens:
        (parts[r + 1],) = backward(r + 1, acts)
    ahead, behind, parts, down_sum, acts = fence(ahead, behind, parts, down_sum, acts)
    ahead, behind, acts, parts = add_and_send(
        half - 1, ahead, behind, acts, parts, halves=True
    )
    for r in evens:
        parts[r] = backward(r, acts, [exchange(parts.pop(r + 1), 1)], pieces)
    parts, down_sum = fence(parts, down_sum)
    down_sum = sum_step(down_sum, 0)
    ahead, behind, parts, down_sum, acts = fence(ahead, behind, parts, down_sum, acts)
    arriving = [partial_gradient(0, parts)]
    ahead, behind, acts = add_and_send(half - 2, ahead, behind, acts)
    down_sum = sum_step(down_sum, 1)
    (parts[1],) = backward(1, acts)
    ahead, behind, parts, arriving, down_sum, acts = fence(
        ahead, behind, parts, arriving, down_sum, acts
    )
    arriving.append(partial_gradient(1, parts))
    for step in range(half - 3, 0, -1):
        ahead, behind, acts = add_and_send(step, ahead, behind, acts)
    down_sum = sum_step(down_sum, 2)
    parts[1] = exchange(parts[1], 1)
    (parts[0],) = backward(0, acts)
    ahead, behind, parts, arriving, down_sum, acts = fence(
        ahead, behind, parts, arriving, down_sum, acts
    )

    base_out = last_add(at, live_rows, total, ahead, behind, n_mp)
    base_out, down_sum, parts, acts = fence(base_out, down_sum, parts, acts)
    base_out = swap_places(base_out)
    branch, *terms = call(
        functools.partial(term_kernel, n_dp, owned),
        "term_up",
        [at, adapter_per_block, live_rows],
        [down_sum, masked_grad, block_up],
        [like((rows, width), BF16)] + [like((rank, width), BF16)] * n_dp,
    )
    terms = [exchange(terms[r], r) if r else terms[0] for r in range(n_dp)]
    arriving.append(partial_gradient(2, parts))
    hidden_gradient = blank((rows, units), BF16)
    for piece in range(2):
        hidden_gradient = combine(
            ends[piece], parts[0], parts[1], arriving[piece], hidden_gradient
        )
    groups = [hidden, near]
    for r in evens:
        groups += [piece[r] for piece in fetched] + [piece[r + 1] for piece in passed]
    down_grad = factor_grad(masks, acts, groups)
    down_grad = jnp.transpose(down_grad.reshape(owned, rank, units), (0, 2, 1))
    terms, hidden_gradient, down_grad, branch = fence(terms, hidden_gradient, down_grad, branch)
    (up_grad,) = call(
        functools.partial(up_grad_kernel, n_dp, blocks),
        "up_grad",
        [at, adapter_per_block],
        terms,
        [like((owned, rank, width), BF16)],
    )
    base_out, arriving[2], up_grad = fence(base_out, arriving[2], up_grad)
    hidden_gradient = combine(ends[2], parts[0], parts[1], arriving[2], hidden_gradient)
    layer_out = (base_out.astype(F32) + branch.astype(F32)).astype(BF16)
    return layer_out, hidden_gradient, down_grad, up_grad


def solution(mesh):
    return jax.shard_map(
        shards,
        mesh=mesh,
        in_specs=(
            P("dp", "mp"),
            P("mp", "dp"),
            P("dp", "mp", None),
            P("dp", None, "mp"),
            P("dp", "mp"),
            P(),
            P(),
        ),
        out_specs=(P("dp", "mp"), P("dp", "mp"), P("dp", "mp", None), P("dp", None, "mp")),
        check_vma=False,
    )
```
